256 devices in a mesh: tm: 64 (over y, z, x_lo), grp: 4 (over x_hi, core).
Axes of the slice: x: 4 (x_hi: 2, x_lo: 2; x = x_hi * 2 + x_lo), y: 4, z: 8, core: 2. Of those that a mesh axis runs over, the one named last changes fastest.
Arguments:
- raw: bfloat16 [2, 262144], P(None, ('tm', 'grp')), may hold values from -7 to 7
- taper: float32 [1024], replicated, may hold values from 0.25 to 1.75
- seg_window: float32 [4096], replicated, may hold values from 0.25 to 1.75
Outputs:
- spectra: float32 [1024, 4096], P(('tm', 'grp'))
The draws below stay inside these ranges and needn't reach their ends.
All inputs are finite; a program needn't handle non-finite values.
Results may differ from the reference program's by a relative error of at most 0.0011.
The reference program's roundings to bfloat16 on the way count: a program that leaves them out, or rounds other values in their place, can miss the bound.
Values may be sent and summed in bfloat16 or wider, within the bound.
A program may use at most 128 MiB of HBM per device.

```python
import math
import jax
import jax.numpy as jnp
from jax import lax

CHANNELS = 1024
NFFT = 4096
SAMPLES = 262144
SEG = 64


def draw_raw(key, part):
    key = jax.random.fold_in(key, 11)
    position = jnp.arange(SAMPLES, dtype=jnp.float32) / SAMPLES
    envelope = 1.7320508 ** (2.0 * position - 1.0)
    values = jnp.clip(jax.random.normal(key, (2, SAMPLES), jnp.float32), -4.0, 4.0)
    return (values * envelope[None, :]).astype(jnp.bfloat16)


def setup_inputs(seed: int = 0) -> dict:
    key_list = jax.random.split(jax.random.key(seed), 4)
    return {
        "raw": draw_raw(jax.random.fold_in(key_list[3], 71), 0),
        "taper": jnp.clip(jax.random.uniform(key_list[1], (CHANNELS,), jnp.float32, 0.25, 1.75), 0.25, 1.75),
        "seg_window": jnp.clip(jax.random.uniform(key_list[2], (NFFT,), jnp.float32, 0.25, 1.75), 0.25, 1.75),
    }


def coefficients(channel_ids, taper):
    tap_count = taper.shape[0]
    tap_ids = jnp.arange(tap_count, dtype=jnp.int32)
    phases = channel_ids[:, None] * tap_ids[None, :] % tap_count
    angle = 2.0 * math.pi / tap_count * phases.astype(jnp.float32)
    weight = taper[None, :] / math.sqrt(tap_count)
    return ((weight * jnp.cos(angle)).astype(jnp.bfloat16), (weight * jnp.sin(angle)).astype(jnp.bfloat16))

def reference(raw, taper, seg_window):
    half_taps = CHANNELS // 2
    stride_len = CHANNELS // 4
    per_seg = NFFT // stride_len
    channel_ids = jnp.arange(CHANNELS, dtype=jnp.int32)
    cosine, sine = coefficients(channel_ids, taper)
    table = jnp.concatenate([jnp.concatenate([cosine.T, -sine.T], 1), jnp.concatenate([sine.T, cosine.T], 1)], 0).astype(jnp.float32)
    raw_float = raw.astype(jnp.float32)
    padded = jnp.pad(raw_float, ((0, 0), (half_taps, half_taps)))
    offsets = jnp.arange(per_seg, dtype=jnp.int32)[:, None] * stride_len + jnp.arange(CHANNELS, dtype=jnp.int32)[None, :]

    def segment(running, seg_index):
        start = seg_index * NFFT
        stretch = lax.dynamic_slice(padded, (jnp.int32(0), start), (2, NFFT + CHANNELS))
        frames = jnp.concatenate([stretch[0][offsets], stretch[1][offsets]], 1)
        chan = jnp.dot(frames, table, precision=lax.Precision.HIGHEST)
        chan = lax.optimization_barrier(chan.astype(jnp.bfloat16)).astype(jnp.float32)
        chan_re = chan[:, None, :CHANNELS]
        chan_im = chan[:, None, CHANNELS:]
        samples = lax.dynamic_slice(raw_float, (jnp.int32(0), start), (2, NFFT))
        samp_re = samples[0].reshape(per_seg, stride_len)[:, :, None]
        samp_im = samples[1].reshape(per_seg, stride_len)[:, :, None]
        weight = seg_window[:, None]
        prod_re = (chan_re * samp_re + chan_im * samp_im).reshape(NFFT, CHANNELS) * weight
        prod_im = (chan_im * samp_re - chan_re * samp_im).reshape(NFFT, CHANNELS) * weight
        estimate = jnp.fft.fft(prod_re + 1j * prod_im, axis=0) / math.sqrt(NFFT)
        power = (jnp.real(estimate) ** 2 + jnp.imag(estimate) ** 2).astype(jnp.float32)
        return (running + power, None)
    running, _ = lax.scan(segment, jnp.zeros((NFFT, CHANNELS), jnp.float32), jnp.arange(SEG, dtype=jnp.int32))
    return (running / SEG).T
```

```python
import math

import jax
import jax.numpy as jnp
import numpy as np
from jax import lax
from jax.experimental import pallas as pl
from jax.experimental.pallas import tpu as pltpu
from jax.sharding import PartitionSpec as P

MESH = pl.DeviceIdType.MESH
F32 = jnp.float32
BF16 = jnp.bfloat16

CHANNELS = 1024
NFFT = 4096
STRIDE = 256
PER_SEG = NFFT // STRIDE
SEG = 64
PLANES, DEPTH, LINE = 4, 8, 8
PLANE_SEG = SEG // PLANES
ROWS = PLANE_SEG * PER_SEG
STRIP = PLANES * LINE * 4
WIDTH = NFFT // LINE


def tables():
    z = np.arange(DEPTH)[:, None, None]
    row = np.arange(STRIP)[None, :, None]
    channel = (row // 32) * 256 + z * 32 + row % 32
    phase = (channel * np.arange(CHANNELS)[None, None, :]) % CHANNELS
    angle = (np.float32(2.0 * math.pi / CHANNELS) * phase.astype(np.float32)).astype(np.float64)
    channel_table = np.concatenate([np.cos(angle), np.sin(angle)], 1).astype(np.float32)
    q = np.arange(LINE)[:, None, None] * WIDTH + np.arange(WIDTH)[None, None, :]
    turn = 2.0 * np.pi / NFFT * ((q * np.arange(STRIDE)[None, :, None]) % NFFT)
    full = np.concatenate([np.cos(turn), -np.sin(turn)], 1)
    high = full.astype(jnp.bfloat16)
    low = (full - high.astype(np.float64)).astype(jnp.bfloat16)
    turn_table = np.stack([high, low], 1)
    j = np.arange(PER_SEG)[:, None]
    step = 2.0 * np.pi / PER_SEG * ((j * np.arange(WIDTH)[None, :]) % PER_SEG)
    step_table = np.stack([np.cos(step), np.sin(step)]).astype(np.float32)
    return channel_table, turn_table, step_table


def kernel(
    raw, taper, window, step_hbm, channel_hbm, turn_hbm, out,
    tile32, tile, buf, halo, rows32, coef32, coef, turn, step, lhs, rhs, acc, blocks, landed,
    local_sem, send_sem, recv_sem,
):
    tm, grp = lax.axis_index("tm"), lax.axis_index("grp")
    y, z, x_lo = tm // 16, lax.rem(tm // 2, DEPTH), lax.rem(tm, 2)
    x_hi, core = grp // 2, lax.rem(grp, 2)
    line = x_lo * 4 + grp
    half = lax.rem(tm, 16) * 2 + x_hi
    place = y * 8 + line

    loads = [
        pltpu.make_async_copy(channel_hbm.at[z], coef32, local_sem.at[0]),
        pltpu.make_async_copy(turn_hbm.at[line], turn, local_sem.at[1]),
        pltpu.make_async_copy(step_hbm, step, local_sem.at[2]),
    ]

    def same_core(i):
        return (y * 16 + i // 2, lax.rem(i, 2) * 2 + core)

    def same_depth(i):
        return ((i // 8 * DEPTH + z) * 2 + lax.rem(i // 4, 2), lax.rem(i, 4))

    partner = (tm, x_hi * 2 + 1 - core)

    barrier = pltpu.get_barrier_semaphore()

    @pl.loop(0, 31)
    def _(i):
        to = same_core(lax.rem(half + 1 + i, 32))
        pl.semaphore_signal(barrier, inc=1, device_id=to, device_id_type=MESH)

    @pl.loop(0, 31)
    def _(i):
        to = same_depth(lax.rem(place + 1 + i, 32))
        pl.semaphore_signal(barrier, inc=1, device_id=to, device_id_type=MESH)

    for load in loads:
        load.start()

    pair = raw[...].astype(F32)
    for part in range(2):
        for chunk in range(8):
            odd, frame = chunk % 2, chunk // 2
            value = pair[part : part + 1, chunk * 128 : (chunk + 1) * 128]
            tile32[0, part * 8 + odd * 4 + frame, :] = value[0]
            tile32[1, part * 8 + (1 - odd) * 4 + frame, :] = value[0]
    tile[...] = jnp.where(core == 0, tile32[0], tile32[1]).astype(BF16)

    @pl.when(y == 0)
    def _():
        halo[0] = jnp.zeros((16, 128), BF16)

    @pl.when(y == PLANES - 1)
    def _():
        halo[1] = jnp.zeros((16, 128), BF16)

    pl.semaphore_wait(barrier, 62)

    own = core * 32 + half
    pltpu.make_async_copy(tile, buf.at[own], recv_sem.at[0]).start()

    @pl.loop(0, 31)
    def _(i):
        pltpu.make_async_remote_copy(
            tile, buf.at[own], send_sem.at[0], recv_sem.at[0],
            device_id=same_core(lax.rem(half + 1 + i, 32)), device_id_type=MESH,
        ).start()

    loads[0].wait()
    for a in range(4):
        for h in range(2):
            i = a * 2 + h
            weight = taper[i : i + 1, :] / math.sqrt(CHANNELS)
            cosine = (weight * coef32[:STRIP, i * 128 : (i + 1) * 128]).astype(BF16)
            sine = (weight * coef32[STRIP:, i * 128 : (i + 1) * 128]).astype(BF16)
            coef[a, :STRIP, h * 128 : (h + 1) * 128] = cosine
            coef[a, STRIP:, h * 128 : (h + 1) * 128] = -sine
            coef[a, :STRIP, 256 + h * 128 : 256 + (h + 1) * 128] = sine
            coef[a, STRIP:, 256 + h * 128 : 256 + (h + 1) * 128] = cosine

    mine = buf.at[pl.ds(core * 32, 32)]
    pltpu.make_async_copy(mine, mine, recv_sem.at[0]).wait()
    forward = pltpu.make_async_remote_copy(
        mine, mine, send_sem.at[1], recv_sem.at[1], device_id=partner, device_id_type=MESH
    )
    forward.start()
    forward.wait_recv()
    sent = buf.at[pl.ds(0, 31)]
    pltpu.make_async_copy(sent, sent, send_sem.at[0]).wait()

    ahead = pltpu.make_async_remote_copy(
        buf.at[63], halo.at[0], send_sem.at[2], recv_sem.at[2],
        device_id=(lax.rem(tm + 16, 64), grp), device_id_type=MESH,
    )
    behind = pltpu.make_async_remote_copy(
        buf.at[0], halo.at[1], send_sem.at[3], recv_sem.at[3],
        device_id=(lax.rem(tm + 48, 64), grp), device_id_type=MESH,
    )

    @pl.when(y < PLANES - 1)
    def _():
        ahead.start()

    @pl.when(y > 0)
    def _():
        behind.start()

    low_rows = lax.broadcasted_iota(jnp.int32, (32, 8, 128), 1) < 4
    for part in range(2):
        first = buf[0:32].astype(F32)[:, part * 8 : part * 8 + 8]
        second = buf[32:64].astype(F32)[:, part * 8 : part * 8 + 8]
        even = jnp.where(low_rows, first, second)
        odd = pltpu.roll(jnp.where(low_rows, second, first), 4, 1)
        rows32[8 : 8 + ROWS, part * 256 : part * 256 + 128] = even.reshape(ROWS, 128)
        rows32[8 : 8 + ROWS, part * 256 + 128 : part * 256 + 256] = odd.reshape(ROWS, 128)

    loads[1].wait()
    loads[2].wait()
    wins = jnp.concatenate(
        [window[pl.ds(0, PER_SEG, stride=2), :], window[pl.ds(1, PER_SEG, stride=2), :]], 1
    ) * (1.0 / 512.0)
    parts = []
    for part in range(2):
        value = rows32[8 : 8 + ROWS, part * 256 : (part + 1) * 256].reshape(PLANE_SEG, PER_SEG, STRIDE)
        parts.append((value * wins[None]).reshape(ROWS, STRIDE))
    samples = jnp.concatenate(
        [jnp.concatenate(parts, 1), jnp.concatenate([-parts[1], parts[0]], 1)], 0
    )
    high = samples.astype(BF16)
    low = (samples - high.astype(F32)).astype(BF16)
    turned = (
        jnp.dot(high, turn[0], preferred_element_type=F32)
        + jnp.dot(high, turn[1], preferred_element_type=F32)
        + jnp.dot(low, turn[0], preferred_element_type=F32)
    )
    g_re = turned[:ROWS].reshape(PLANE_SEG, PER_SEG, WIDTH)
    g_im = turned[ROWS:].reshape(PLANE_SEG, PER_SEG, WIDTH)
    cos_step, sin_step = step[0][None], step[1][None]
    for i, value in enumerate((g_re * cos_step + g_im * sin_step, g_im * cos_step - g_re * sin_step)):
        top = value.astype(BF16)
        rhs[:, i * 16 : i * 16 + 16, :] = top
        rhs[:, 32 + i * 16 : 48 + i * 16, :] = (value - top.astype(F32)).astype(BF16)

    @pl.when(y > 0)
    def _():
        ahead.wait_recv()

    @pl.when(y < PLANES - 1)
    def _():
        behind.wait_recv()

    before, after = halo[0].astype(F32), halo[1].astype(F32)
    for part in range(2):
        at = part * 256
        rows32[6:8, at : at + 128] = before[part * 8 + 6 : part * 8 + 8]
        rows32[6:8, at + 128 : at + 256] = before[part * 8 + 2 : part * 8 + 4]
        rows32[8 + ROWS : 9 + ROWS, at : at + 128] = after[part * 8 : part * 8 + 1]
        rows32[8 + ROWS : 9 + ROWS, at + 128 : at + 256] = after[part * 8 + 4 : part * 8 + 5]
    frames = jnp.zeros((ROWS, 2 * STRIP), F32)
    for a in range(4):
        frames += lax.dot_general(
            rows32[6 + a : 6 + a + ROWS, :].astype(BF16), coef[a],
            (((1,), (1,)), ((), ())), preferred_element_type=F32,
        )
    rounded = frames.astype(BF16)
    swapped = jnp.concatenate([-rounded[:, STRIP:], rounded[:, :STRIP]], 1)
    for i, value in enumerate((rounded, swapped, rounded, swapped)):
        lhs[:, i * 16 : i * 16 + 16, :] = value.reshape(PLANE_SEG, PER_SEG, 2 * STRIP)

    acc[...] = jnp.zeros_like(acc)

    @pl.loop(0, PLANE_SEG)
    def _(s):
        estimate = lax.dot_general(
            lhs[s], rhs[s], (((0,), (0,)), ((), ())), preferred_element_type=F32
        )
        acc[...] += estimate[:STRIP] * estimate[:STRIP] + estimate[STRIP:] * estimate[STRIP:]

    low_half = lax.broadcasted_iota(jnp.int32, (16, 8, 256), 1) < 4
    left = acc[:, :256].reshape(16, 8, 256)
    right = acc[:, 256:].reshape(16, 8, 256)
    even = jnp.where(low_half, left, pltpu.roll(right, 4, 1))
    odd = jnp.where(low_half, pltpu.roll(left, 4, 1), right)
    for t in range(16):
        blocks[2 * t] = even[t]
        blocks[2 * t + 1] = odd[t]

    pltpu.make_async_copy(blocks.at[place], landed.at[place], recv_sem.at[4]).start()

    @pl.loop(0, 31)
    def _(i):
        to = lax.rem(place + 1 + i, 32)
        pltpu.make_async_remote_copy(
            blocks.at[to], landed.at[place], send_sem.at[4], recv_sem.at[4],
            device_id=same_depth(to), device_id_type=MESH,
        ).start()

    pltpu.make_async_copy(landed, landed, recv_sem.at[4]).wait()
    for i in range(LINE):
        total = landed[i] + landed[8 + i] + landed[16 + i] + landed[24 + i]
        out[:, i * WIDTH : i * WIDTH + 256] = total[0:4]
        out[:, i * WIDTH + 256 : (i + 1) * WIDTH] = total[4:8]

    forward.wait_send()

    @pl.when(y < PLANES - 1)
    def _():
        ahead.wait_send()

    @pl.when(y > 0)
    def _():
        behind.wait_send()

    gone = blocks.at[pl.ds(0, 31)]
    pltpu.make_async_copy(gone, gone, send_sem.at[4]).wait()


def body(raw, taper, seg_window):
    channel_table, turn_table, step_table = tables()
    vmem = pl.BlockSpec(memory_space=pltpu.VMEM)
    hbm = pl.BlockSpec(memory_space=pl.ANY)
    return pl.pallas_call(
        kernel,
        out_shape=jax.ShapeDtypeStruct((4, NFFT), F32),
        in_specs=[vmem, vmem, vmem, hbm, hbm, hbm],
        out_specs=vmem,
        scratch_shapes=[
            pltpu.VMEM((2, 16, 128), F32),
            pltpu.VMEM((16, 128), BF16),
            pltpu.VMEM((64, 16, 128), BF16),
            pltpu.VMEM((2, 16, 128), BF16),
            pltpu.VMEM((ROWS + 16, 512), F32),
            pltpu.VMEM((2 * STRIP, CHANNELS), F32),
            pltpu.VMEM((4, 2 * STRIP, 512), BF16),
            pltpu.VMEM((2, 512, WIDTH), BF16),
            pltpu.VMEM((2, PER_SEG, WIDTH), F32),
            pltpu.VMEM((PLANE_SEG, 64, 2 * STRIP), BF16),
            pltpu.VMEM((PLANE_SEG, 64, WIDTH), BF16),
            pltpu.VMEM((STRIP, WIDTH), F32),
            pltpu.VMEM((32, 8, 256), F32),
            pltpu.VMEM((32, 8, 256), F32),
            pltpu.SemaphoreType.DMA((3,)),
            pltpu.SemaphoreType.DMA((5,)),
            pltpu.SemaphoreType.DMA((5,)),
        ],
        compiler_params=pltpu.CompilerParams(
            collective_id=0, has_side_effects=True, vmem_limit_bytes=48 * 1024 * 1024
        ),
    )(
        raw, taper.reshape(8, 128), seg_window.reshape(32, 128),
        jnp.asarray(step_table), jnp.asarray(channel_table), jnp.asarray(turn_table),
    )


def solution(mesh):
    placed = (P(None, ("tm", "grp")), P(), P())
    return jax.shard_map(
        body, mesh=mesh, in_specs=placed, out_specs=P(("tm", "grp"), None), check_vma=False
    )
```

```python
import math

import jax
import jax.numpy as jnp
import numpy as np
from jax import lax
from jax.experimental import pallas as pl
from jax.experimental.pallas import tpu as pltpu
from jax.sharding import PartitionSpec as P

MESH = pl.DeviceIdType.MESH
F32 = jnp.float32
BF16 = jnp.bfloat16

CHANNELS = 1024
NFFT = 4096
STRIDE = 256
PER_SEG = NFFT // STRIDE
SEG = 64
PLANES, DEPTH, LINE = 4, 8, 8
PLANE_SEG = SEG // PLANES
ROWS = PLANE_SEG * PER_SEG
HALF_ROWS = ROWS // 2
STRIP = PLANES * LINE * 4
WIDTH = NFFT // LINE
HOPS = (0, 1, 2, 1)
MEMBERS = sorted(((dx, dc) for dx in range(4) for dc in range(2) if dx or dc), key=lambda m: -HOPS[m[0]])
OWNERS = sorted(
    ((dy, dx, dc) for dy in range(4) for dx in range(4) for dc in range(2) if dy or dx or dc),
    key=lambda m: -(HOPS[m[0]] + HOPS[m[1]]),
)


def tables():
    z = np.arange(DEPTH)[:, None, None]
    row = np.arange(STRIP)[None, :, None]
    channel = (row // 32) * 256 + z * 32 + row % 32
    phase = (channel * np.arange(CHANNELS)[None, None, :]) % CHANNELS
    angle = (np.float32(2.0 * math.pi / CHANNELS) * phase.astype(np.float32)).astype(np.float64)
    channel_table = np.concatenate([np.cos(angle), np.sin(angle)], 1).astype(np.float32)
    q = np.arange(LINE)[:, None, None] * WIDTH + np.arange(WIDTH)[None, None, :]
    turn = 2.0 * np.pi / NFFT * ((q * np.arange(STRIDE)[None, :, None]) % NFFT)
    full = np.concatenate([np.cos(turn), -np.sin(turn)], 1)
    high = full.astype(jnp.bfloat16)
    low = (full - high.astype(np.float64)).astype(jnp.bfloat16)
    turn_table = np.stack([high, low], 1)
    j = np.arange(PER_SEG)[:, None]
    step = 2.0 * np.pi / PER_SEG * ((j * np.arange(WIDTH)[None, :]) % PER_SEG)
    step_table = np.stack([np.cos(step), np.sin(step)]).astype(np.float32)
    return channel_table, turn_table, step_table


def kernel(
    raw_hbm, taper_hbm, window_hbm, step_hbm, channel_hbm, turn_hbm, out,
    raw, taper, window, tile32, buf, halo, rows32, coef32, coef, turn, step, lhs, rhs, acc, blocks, landed,
    local_sem, send_sem, recv_sem,
):
    tm, grp = lax.axis_index("tm"), lax.axis_index("grp")
    y, z, x_lo = tm // 16, lax.rem(tm // 2, DEPTH), lax.rem(tm, 2)
    x, core = grp // 2 * 2 + x_lo, lax.rem(grp, 2)
    line = x_lo * 4 + grp
    mine, other = z // 4, 1 - z // 4
    zz = lax.rem(z, 4)
    place = y * 8 + line

    xs = [lax.rem(x + d, 4) for d in range(4)]
    ys = [lax.rem(y + d, PLANES) for d in range(PLANES)]
    cores = [core, 1 - core]

    def member(dx, dc):
        return lax.rem(xs[dx], 2) * 4 + xs[dx] // 2 * 2 + cores[dc]

    def at(plane, depth, member):
        return ((plane * DEPTH + depth) * 2 + member // 4, lax.rem(member, 4))

    def send(src, dst, send_at, recv_at, to):
        pltpu.make_async_remote_copy(
            src, dst, send_sem.at[send_at], recv_sem.at[recv_at],
            device_id=to, device_id_type=MESH,
        ).start()

    def arrived(ref, sem):
        pltpu.make_async_copy(ref, ref, sem).wait()

    loads = [
        pltpu.make_async_copy(raw_hbm, raw, local_sem.at[0]),
        pltpu.make_async_copy(taper_hbm, taper, local_sem.at[1]),
        pltpu.make_async_copy(channel_hbm.at[z], coef32, local_sem.at[2]),
        pltpu.make_async_copy(window_hbm, window, local_sem.at[3]),
        pltpu.make_async_copy(step_hbm, step, local_sem.at[4]),
        pltpu.make_async_copy(turn_hbm.at[line], turn, local_sem.at[5]),
    ]
    loads[0].start()

    barrier = pltpu.get_barrier_semaphore()

    def greet(to):
        pl.semaphore_signal(barrier, inc=1, device_id=to, device_id_type=MESH)

    @pl.when(mine == 0)
    def _():
        for i in range(4):
            greet(at(y, 4 + i, line))

    for i in range(1, 4):
        greet(at(y, mine * 4 + lax.rem(zz + i, 4), line))

    for dx, dc in MEMBERS:
        greet(at(y, z, member(dx, dc)))
    for i in range(1, PLANES):
        greet(at(ys[i], z, line))

    for load in loads[1:]:
        load.start()

    loads[0].wait()
    pair = raw[...].astype(F32)
    for part in range(2):
        for chunk in range(8):
            odd, frame = chunk % 2, chunk // 2
            value = pair[part : part + 1, chunk * 128 : (chunk + 1) * 128]
            tile32[0, part * 8 + odd * 4 + frame, :] = value[0]
            tile32[1, part * 8 + (1 - odd) * 4 + frame, :] = value[0]
    own = (mine * 8 + line) * 4 + zz
    buf[own] = jnp.where(core == 0, tile32[0], tile32[1]).astype(BF16)

    @pl.when(y == 0)
    def _():
        halo[0] = jnp.zeros((16, 128), BF16)

    @pl.when(y == PLANES - 1)
    def _():
        halo[1] = jnp.zeros((16, 128), BF16)

    @pl.when(mine == 0)
    def _():
        pl.semaphore_wait(barrier, 13)

    @pl.when(mine == 1)
    def _():
        pl.semaphore_wait(barrier, 17)

    def along_z_far():
        for i in range(4):
            send(buf.at[own], buf.at[own], 0, 1, at(y, other * 4 + i, line))

    def along_x(part, send_at, recv_at):
        block = buf.at[pl.ds((part * 8 + line) * 4, 4)]
        for dx, dc in MEMBERS:
            send(block, block, send_at, recv_at, at(y, z, member(dx, dc)))

    def ends(part):
        @pl.when((part == 0) & (line == 0) & (y > 0))
        def _():
            for i in range(8):
                send(buf.at[0], halo.at[1], 3, 5, at(y - 1, z, i))

        @pl.when((part == 1) & (line == 7) & (y < PLANES - 1))
        def _():
            for i in range(8):
                send(buf.at[63], halo.at[0], 3, 4, at(y + 1, z, i))

    @pl.when(mine == 1)
    def _():
        along_z_far()

    for i in range(1, 4):
        send(buf.at[own], buf.at[own], 0, 0, at(y, mine * 4 + lax.rem(zz + i, 4), line))

    loads[1].wait()
    loads[2].wait()
    for a in range(4):
        for h in range(2):
            i = a * 2 + h
            weight = taper[i : i + 1, :] / math.sqrt(CHANNELS)
            cosine = (weight * coef32[:STRIP, i * 128 : (i + 1) * 128]).astype(BF16)
            sine = (weight * coef32[STRIP:, i * 128 : (i + 1) * 128]).astype(BF16)
            coef[a, :STRIP, h * 128 : (h + 1) * 128] = cosine
            coef[a, STRIP:, h * 128 : (h + 1) * 128] = -sine
            coef[a, :STRIP, 256 + h * 128 : 256 + (h + 1) * 128] = sine
            coef[a, STRIP:, 256 + h * 128 : 256 + (h + 1) * 128] = cosine

    arrived(buf.at[pl.ds(0, 3)], recv_sem.at[0])
    along_x(mine, 1, 2)
    for load in loads[3:]:
        load.wait()

    wins = jnp.concatenate(
        [window[pl.ds(0, PER_SEG, stride=2), :], window[pl.ds(1, PER_SEG, stride=2), :]], 1
    ) * (1.0 / 512.0)
    low_rows = lax.broadcasted_iota(jnp.int32, (4, 8, 128), 1) < 4

    def arrange(part):
        start = pl.multiple_of(8 + part * HALF_ROWS, 8)
        for p in range(2):
            evens, odds = [], []
            for i in range(4):
                first = buf[pl.ds((part * 8 + 2 * i) * 4, 4)].astype(F32)[:, p * 8 : p * 8 + 8]
                second = buf[pl.ds((part * 8 + 2 * i + 1) * 4, 4)].astype(F32)[:, p * 8 : p * 8 + 8]
                evens.append(jnp.where(low_rows, first, second))
                odds.append(pltpu.roll(jnp.where(low_rows, second, first), 4, 1))
            for h, pieces in enumerate((evens, odds)):
                at_lane = p * 256 + h * 128
                rows32[pl.ds(start, HALF_ROWS), at_lane : at_lane + 128] = jnp.stack(pieces, 1).reshape(HALF_ROWS, 128)

    def short_transforms(part):
        start = pl.multiple_of(8 + part * HALF_ROWS, 8)
        parts = []
        for p in range(2):
            value = rows32[pl.ds(start, HALF_ROWS), p * 256 : (p + 1) * 256].reshape(8, PER_SEG, STRIDE)
            parts.append((value * wins[None]).reshape(HALF_ROWS, STRIDE))
        samples = jnp.concatenate(
            [jnp.concatenate(parts, 1), jnp.concatenate([-parts[1], parts[0]], 1)], 0
        )
        high = samples.astype(BF16)
        low = (samples - high.astype(F32)).astype(BF16)
        turned = (
            jnp.dot(high, turn[0], preferred_element_type=F32)
            + jnp.dot(high, turn[1], preferred_element_type=F32)
            + jnp.dot(low, turn[0], preferred_element_type=F32)
        )
        g_re = turned[:HALF_ROWS].reshape(8, PER_SEG, WIDTH)
        g_im = turned[HALF_ROWS:].reshape(8, PER_SEG, WIDTH)
        cos_step, sin_step = step[0][None], step[1][None]
        for i, value in enumerate((g_re * cos_step + g_im * sin_step, g_im * cos_step - g_re * sin_step)):
            top = value.astype(BF16)
            rhs[pl.ds(part * 8, 8), i * 16 : i * 16 + 16, :] = top
            rhs[pl.ds(part * 8, 8), 32 + i * 16 : 48 + i * 16, :] = (value - top.astype(F32)).astype(BF16)

    def frames(runs):
        total = None
        for a in range(4):
            pieces = []
            for first, count in runs:
                start = pl.multiple_of(first * PER_SEG, 8)
                chunk = rows32[pl.ds(start, (count + 1) * PER_SEG), :]
                pieces.append(chunk[6 + a : 6 + a + count * PER_SEG].astype(BF16))
            term = lax.dot_general(
                jnp.concatenate(pieces, 0), coef[a], (((1,), (1,)), ((), ())), preferred_element_type=F32
            )
            total = term if total is None else total + term
        rounded = total.astype(BF16).astype(F32)
        swapped = jnp.concatenate([-rounded[:, STRIP:], rounded[:, :STRIP]], 1)
        row = 0
        for first, count in runs:
            for s in range(count):
                pair = jnp.concatenate([rounded[row : row + PER_SEG], swapped[row : row + PER_SEG]], 0)
                lhs[first + s] = jnp.concatenate([pair, pair], 0).T.astype(BF16)
                row += PER_SEG

    def power(segments, first):
        for n in range(2):
            lanes = slice(n * 256, (n + 1) * 256)
            total = None if first else acc[:, lanes]
            for s in segments:
                e = jnp.dot(lhs[s], rhs[s][:, lanes], preferred_element_type=F32)
                term = e[:STRIP] * e[:STRIP] + e[STRIP:] * e[STRIP:]
                total = term if total is None else total + term
            acc[:, lanes] = total

    arrived(buf.at[pl.ds(0, 28)], recv_sem.at[2])
    ends(mine)
    arrange(mine)
    short_transforms(mine)
    frames([(mine * 8 + 1, 6)])
    power([mine * 8 + s for s in range(1, 7)], True)

    arrived(buf.at[pl.ds(0, 4)], recv_sem.at[1])
    along_x(other, 2, 3)
    ends(other)

    @pl.when(mine == 0)
    def _():
        along_z_far()

    arrived(buf.at[pl.ds(0, 28)], recv_sem.at[3])

    @pl.when(y > 0)
    def _():
        arrived(halo.at[0], recv_sem.at[4])

    @pl.when(y < PLANES - 1)
    def _():
        arrived(halo.at[1], recv_sem.at[5])

    before, after = halo[0].astype(F32), halo[1].astype(F32)
    for p in range(2):
        lane = p * 256
        rows32[6:8, lane : lane + 128] = before[p * 8 + 6 : p * 8 + 8]
        rows32[6:8, lane + 128 : lane + 256] = before[p * 8 + 2 : p * 8 + 4]
        rows32[8 + ROWS : 9 + ROWS, lane : lane + 128] = after[p * 8 : p * 8 + 1]
        rows32[8 + ROWS : 9 + ROWS, lane + 128 : lane + 256] = after[p * 8 + 4 : p * 8 + 5]
    arrange(other)
    short_transforms(other)
    frames([(mine * 8, 1), (mine * 8 + 7, 1), (other * 8, 8)])
    power([mine * 8, mine * 8 + 7] + [other * 8 + s for s in range(8)], False)

    low_half = lax.broadcasted_iota(jnp.int32, (16, 8, 256), 1) < 4
    left = acc[:, :256].reshape(16, 8, 256)
    right = acc[:, 256:].reshape(16, 8, 256)
    even = jnp.where(low_half, left, pltpu.roll(right, 4, 1))
    odd = jnp.where(low_half, pltpu.roll(left, 4, 1), right)
    for t in range(16):
        blocks[2 * t] = even[t]
        blocks[2 * t + 1] = odd[t]

    for dy, dx, dc in OWNERS:
        to = ys[dy] * 8 + member(dx, dc)
        send(blocks.at[to], landed.at[place], 4, 6, at(ys[dy], z, member(dx, dc)))

    landed[place] = blocks[place]
    arrived(landed.at[pl.ds(0, 31)], recv_sem.at[6])
    for i in range(LINE):
        total = landed[i] + landed[8 + i] + landed[16 + i] + landed[24 + i]
        out[:, i * WIDTH : i * WIDTH + 256] = total[0:4]
        out[:, i * WIDTH + 256 : (i + 1) * WIDTH] = total[4:8]

    arrived(buf.at[pl.ds(0, 7)], send_sem.at[0])
    arrived(buf.at[pl.ds(0, 28)], send_sem.at[1])
    arrived(buf.at[pl.ds(0, 28)], send_sem.at[2])

    @pl.when((line == 0) & (y > 0))
    def _():
        arrived(buf.at[pl.ds(0, 8)], send_sem.at[3])

    @pl.when((line == 7) & (y < PLANES - 1))
    def _():
        arrived(buf.at[pl.ds(0, 8)], send_sem.at[3])

    arrived(blocks.at[pl.ds(0, 31)], send_sem.at[4])


def body(raw, taper, seg_window):
    channel_table, turn_table, step_table = tables()
    operands = (
        raw, taper.reshape(8, 128), seg_window.reshape(32, 128),
        jnp.asarray(step_table), jnp.asarray(channel_table), jnp.asarray(turn_table),
    )
    vmem = pl.BlockSpec(memory_space=pltpu.VMEM)
    hbm = pl.BlockSpec(memory_space=pltpu.HBM)
    return pl.pallas_call(
        kernel,
        out_shape=jax.ShapeDtypeStruct((4, NFFT), F32),
        in_specs=[hbm] * 6,
        out_specs=vmem,
        scratch_shapes=[
            pltpu.VMEM((2, 1024), BF16),
            pltpu.VMEM((8, 128), F32),
            pltpu.VMEM((32, 128), F32),
            pltpu.VMEM((2, 16, 128), F32),
            pltpu.VMEM((64, 16, 128), BF16),
            pltpu.VMEM((2, 16, 128), BF16),
            pltpu.VMEM((ROWS + 16, 512), F32),
            pltpu.VMEM((2 * STRIP, CHANNELS), F32),
            pltpu.VMEM((4, 2 * STRIP, 512), BF16),
            pltpu.VMEM((2, 512, WIDTH), BF16),
            pltpu.VMEM((2, PER_SEG, WIDTH), F32),
            pltpu.VMEM((PLANE_SEG, 2 * STRIP, 64), BF16),
            pltpu.VMEM((PLANE_SEG, 64, WIDTH), BF16),
            pltpu.VMEM((STRIP, WIDTH), F32),
            pltpu.VMEM((32, 8, 256), F32),
            pltpu.VMEM((32, 8, 256), F32),
            pltpu.SemaphoreType.DMA((6,)),
            pltpu.SemaphoreType.DMA((5,)),
            pltpu.SemaphoreType.DMA((7,)),
        ],
        compiler_params=pltpu.CompilerParams(
            collective_id=0, has_side_effects=True, vmem_limit_bytes=48 * 1024 * 1024
        ),
    )(*(pltpu.with_memory_space_constraint(x, pltpu.HBM) for x in operands))


def solution(mesh):
    placed = (P(None, ("tm", "grp")), P(), P())
    return jax.shard_map(
        body, mesh=mesh, in_specs=placed, out_specs=P(("tm", "grp"), None), check_vma=False
    )
```

```python
import math

import jax
import jax.numpy as jnp
import numpy as np
from jax import lax
from jax.experimental import pallas as pl
from jax.experimental.pallas import tpu as pltpu
from jax.sharding import PartitionSpec as P

MESH = pl.DeviceIdType.MESH
F32 = jnp.float32
BF16 = jnp.bfloat16

CHANNELS = 1024
NFFT = 4096
STRIDE = 256
PER_SEG = NFFT // STRIDE
SEG = 64
PLANES, DEPTH, LINE = 4, 8, 8
PLANE_SEG = SEG // PLANES
ROWS = PLANE_SEG * PER_SEG
HALF_ROWS = ROWS // 2
STRIP = PLANES * LINE * 4
WIDTH = NFFT // LINE
HOPS = (0, 1, 2, 1)
MEMBERS = sorted(((dx, dc) for dx in range(4) for dc in range(2) if dx or dc), key=lambda m: -HOPS[m[0]])
OWNERS = sorted(
    ((dy, dx, dc) for dy in range(4) for dx in range(4) for dc in range(2) if dy or dx or dc),
    key=lambda m: -(HOPS[m[0]] + HOPS[m[1]]),
)


def tables():
    z = np.arange(DEPTH)[:, None, None]
    row = np.arange(STRIP)[None, :, None]
    channel = (row // 32) * 256 + z * 32 + row % 32
    phase = (channel * np.arange(CHANNELS)[None, None, :]) % CHANNELS
    angle = (np.float32(2.0 * math.pi / CHANNELS) * phase.astype(np.float32)).astype(np.float64)
    channel_table = np.concatenate([np.cos(angle), np.sin(angle)], 1).astype(np.float32)
    q = np.arange(LINE)[:, None, None] * WIDTH + np.arange(WIDTH)[None, None, :]
    turn = 2.0 * np.pi / NFFT * ((q * np.arange(STRIDE)[None, :, None]) % NFFT)
    full = np.concatenate([np.cos(turn), -np.sin(turn)], 1)
    high = full.astype(jnp.bfloat16)
    low = (full - high.astype(np.float64)).astype(jnp.bfloat16)
    turn_table = np.stack([high, low], 1)
    j = np.arange(PER_SEG)[:, None]
    step = 2.0 * np.pi / PER_SEG * ((j * np.arange(WIDTH)[None, :]) % PER_SEG)
    step_table = np.stack([np.cos(step), np.sin(step)]).astype(np.float32)
    return channel_table, turn_table, step_table


def kernel(
    raw_hbm, taper_hbm, window_hbm, step_hbm, channel_hbm, turn_hbm, out,
    raw, taper, window, tile32, buf, halo, rows32, coef32, coef, turn, step, lhs, rhs, acc, blocks, landed,
    local_sem, send_sem, recv_sem,
):
    tm, grp = lax.axis_index("tm"), lax.axis_index("grp")
    y, z, x_lo = tm // 16, lax.rem(tm // 2, DEPTH), lax.rem(tm, 2)
    x, core = grp // 2 * 2 + x_lo, lax.rem(grp, 2)
    line = x_lo * 4 + grp
    mine, other = z // 4, 1 - z // 4
    zz = lax.rem(z, 4)
    place = y * 8 + line

    xs = [lax.rem(x + d, 4) for d in range(4)]
    ys = [lax.rem(y + d, PLANES) for d in range(PLANES)]
    cores = [core, 1 - core]

    def member(dx, dc):
        return lax.rem(xs[dx], 2) * 4 + xs[dx] // 2 * 2 + cores[dc]

    def at(plane, depth, member):
        return ((plane * DEPTH + depth) * 2 + member // 4, lax.rem(member, 4))

    def send(src, dst, send_at, recv_at, to):
        pltpu.make_async_remote_copy(
            src, dst, send_sem.at[send_at], recv_sem.at[recv_at],
            device_id=to, device_id_type=MESH,
        ).start()

    def arrived(ref, sem):
        pltpu.make_async_copy(ref, ref, sem).wait()

    loads = [
        pltpu.make_async_copy(raw_hbm, raw, local_sem.at[0]),
        pltpu.make_async_copy(taper_hbm, taper, local_sem.at[1]),
        pltpu.make_async_copy(channel_hbm.at[z], coef32, local_sem.at[2]),
        pltpu.make_async_copy(window_hbm, window, local_sem.at[3]),
        pltpu.make_async_copy(step_hbm, step, local_sem.at[4]),
        pltpu.make_async_copy(turn_hbm.at[line], turn, local_sem.at[5]),
    ]
    loads[0].start()

    barrier = pltpu.get_barrier_semaphore()

    def greet(to):
        pl.semaphore_signal(barrier, inc=1, device_id=to, device_id_type=MESH)

    @pl.when(mine == 0)
    def _():
        for i in range(4):
            greet(at(y, 4 + i, line))

    for i in range(1, 4):
        greet(at(y, mine * 4 + lax.rem(zz + i, 4), line))

    for dx, dc in MEMBERS:
        greet(at(y, z, member(dx, dc)))
    for i in range(1, PLANES):
        greet(at(ys[i], z, line))

    loads[0].wait()
    pair = raw[...].astype(F32)
    for part in range(2):
        for chunk in range(8):
            odd, frame = chunk % 2, chunk // 2
            value = pair[part : part + 1, chunk * 128 : (chunk + 1) * 128]
            tile32[0, part * 8 + odd * 4 + frame, :] = value[0]
            tile32[1, part * 8 + (1 - odd) * 4 + frame, :] = value[0]
    own = (mine * 8 + line) * 4 + zz
    buf[own] = jnp.where(core == 0, tile32[0], tile32[1]).astype(BF16)

    @pl.when(y == 0)
    def _():
        halo[0] = jnp.zeros((16, 128), BF16)

    @pl.when(y == PLANES - 1)
    def _():
        halo[1] = jnp.zeros((16, 128), BF16)

    @pl.when(mine == 0)
    def _():
        pl.semaphore_wait(barrier, 13)

    @pl.when(mine == 1)
    def _():
        pl.semaphore_wait(barrier, 17)

    def along_x(part, send_at, recv_at):
        block = buf.at[pl.ds((part * 8 + line) * 4, 4)]
        for dx, dc in MEMBERS:
            send(block, block, send_at, recv_at, at(y, z, member(dx, dc)))

    def ends(part):
        @pl.when((part == 0) & (line == 0) & (y > 0))
        def _():
            for i in range(8):
                send(buf.at[0], halo.at[1], 3, 5, at(y - 1, z, i))

        @pl.when((part == 1) & (line == 7) & (y < PLANES - 1))
        def _():
            for i in range(8):
                send(buf.at[63], halo.at[0], 3, 4, at(y + 1, z, i))

    @pl.when(mine == 1)
    def _():
        for i in range(4):
            send(buf.at[own], buf.at[own], 0, 7 + zz, at(y, i, line))

    for i in range(1, 4):
        send(buf.at[own], buf.at[own], 0, 0, at(y, mine * 4 + lax.rem(zz + i, 4), line))

    for load in loads[1:]:
        load.start()

    loads[1].wait()
    loads[2].wait()
    for a in range(4):
        for h in range(2):
            i = a * 2 + h
            weight = taper[i : i + 1, :] / math.sqrt(CHANNELS)
            cosine = (weight * coef32[:STRIP, i * 128 : (i + 1) * 128]).astype(BF16)
            sine = (weight * coef32[STRIP:, i * 128 : (i + 1) * 128]).astype(BF16)
            coef[a, :STRIP, h * 128 : (h + 1) * 128] = cosine
            coef[a, STRIP:, h * 128 : (h + 1) * 128] = -sine
            coef[a, :STRIP, 256 + h * 128 : 256 + (h + 1) * 128] = sine
            coef[a, STRIP:, 256 + h * 128 : 256 + (h + 1) * 128] = cosine

    arrived(buf.at[pl.ds(0, 3)], recv_sem.at[0])
    along_x(mine, 1, 2)
    for load in loads[3:]:
        load.wait()

    wins = jnp.concatenate(
        [window[pl.ds(0, PER_SEG, stride=2), :], window[pl.ds(1, PER_SEG, stride=2), :]], 1
    ) * (1.0 / 512.0)
    low_rows = lax.broadcasted_iota(jnp.int32, (4, 8, 128), 1) < 4

    def arrange(part):
        start = pl.multiple_of(8 + part * HALF_ROWS, 8)
        for p in range(2):
            evens, odds = [], []
            for i in range(4):
                first = buf[pl.ds((part * 8 + 2 * i) * 4, 4)].astype(F32)[:, p * 8 : p * 8 + 8]
                second = buf[pl.ds((part * 8 + 2 * i + 1) * 4, 4)].astype(F32)[:, p * 8 : p * 8 + 8]
                evens.append(jnp.where(low_rows, first, second))
                odds.append(pltpu.roll(jnp.where(low_rows, second, first), 4, 1))
            for h, pieces in enumerate((evens, odds)):
                at_lane = p * 256 + h * 128
                rows32[pl.ds(start, HALF_ROWS), at_lane : at_lane + 128] = jnp.stack(pieces, 1).reshape(HALF_ROWS, 128)

    def short_transforms(part):
        start = pl.multiple_of(8 + part * HALF_ROWS, 8)
        parts = []
        for p in range(2):
            value = rows32[pl.ds(start, HALF_ROWS), p * 256 : (p + 1) * 256].reshape(8, PER_SEG, STRIDE)
            parts.append((value * wins[None]).reshape(HALF_ROWS, STRIDE))
        samples = jnp.concatenate(
            [jnp.concatenate(parts, 1), jnp.concatenate([-parts[1], parts[0]], 1)], 0
        )
        high = samples.astype(BF16)
        low = (samples - high.astype(F32)).astype(BF16)
        turned = (
            jnp.dot(high, turn[0], preferred_element_type=F32)
            + jnp.dot(high, turn[1], preferred_element_type=F32)
            + jnp.dot(low, turn[0], preferred_element_type=F32)
        )
        g_re = turned[:HALF_ROWS].reshape(8, PER_SEG, WIDTH)
        g_im = turned[HALF_ROWS:].reshape(8, PER_SEG, WIDTH)
        cos_step, sin_step = step[0][None], step[1][None]
        for i, value in enumerate((g_re * cos_step + g_im * sin_step, g_im * cos_step - g_re * sin_step)):
            top = value.astype(BF16)
            rhs[pl.ds(part * 8, 8), i * 16 : i * 16 + 16, :] = top
            rhs[pl.ds(part * 8, 8), 32 + i * 16 : 48 + i * 16, :] = (value - top.astype(F32)).astype(BF16)

    def frames(runs):
        pieces = []
        for first, count in runs:
            start = pl.multiple_of(first * PER_SEG, 16)
            pieces.append(rows32[pl.ds(start, (count + 1) * PER_SEG), :].astype(BF16))
        rows = jnp.concatenate(pieces, 0)
        total = None
        for a in range(4):
            term = lax.dot_general(rows, coef[a], (((1,), (1,)), ((), ())), preferred_element_type=F32)
            taken, row = [], 6 + a
            for first, count in runs:
                taken.append(term[row : row + count * PER_SEG])
                row += (count + 1) * PER_SEG
            term = jnp.concatenate(taken, 0)
            total = term if total is None else total + term
        rounded = total.astype(BF16).astype(F32)
        swapped = jnp.concatenate([-rounded[:, STRIP:], rounded[:, :STRIP]], 1)
        row = 0
        for first, count in runs:
            for s in range(count):
                pair = jnp.concatenate([rounded[row : row + PER_SEG], swapped[row : row + PER_SEG]], 0)
                lhs[first + s] = jnp.concatenate([pair, pair], 0).T.astype(BF16)
                row += PER_SEG

    def power(segments, first):
        for n in range(2):
            lanes = slice(n * 256, (n + 1) * 256)
            total = None if first else acc[:, lanes]
            for s in segments:
                e = jnp.dot(lhs[s], rhs[s][:, lanes], preferred_element_type=F32)
                term = e[:STRIP] * e[:STRIP] + e[STRIP:] * e[STRIP:]
                total = term if total is None else total + term
            acc[:, lanes] = total

    arrived(buf.at[pl.ds(0, 28)], recv_sem.at[2])
    ends(mine)

    def late_tile(i):
        arrived(buf.at[0], recv_sem.at[7 + i])

    def early_block(i):
        block = buf.at[pl.ds(line * 4, 4)]
        send(block, block, 5, 1, at(y, 4 + i, line))

    @pl.when(z == 0)
    def _():
        for i in (3, 2):
            late_tile(i)
            early_block(i)
        late_tile(1)
        late_tile(0)

    @pl.when(z == 3)
    def _():
        for i in (0, 1):
            late_tile(i)
            early_block(i)
        late_tile(2)
        late_tile(3)

    @pl.when((z == 1) | (z == 2))
    def _():
        for i in range(4):
            late_tile(i)

    @pl.when(mine == 1)
    def _():
        arrived(buf.at[pl.ds(0, 4)], recv_sem.at[1])

    along_x(other, 2, 3)
    ends(other)

    arrange(mine)
    short_transforms(mine)
    frames([(mine * 8 + 1, 6)])
    power([mine * 8 + s for s in range(1, 7)], True)

    arrived(buf.at[pl.ds(0, 28)], recv_sem.at[3])

    @pl.when(y > 0)
    def _():
        arrived(halo.at[0], recv_sem.at[4])

    @pl.when(y < PLANES - 1)
    def _():
        arrived(halo.at[1], recv_sem.at[5])

    before, after = halo[0].astype(F32), halo[1].astype(F32)
    for p in range(2):
        lane = p * 256
        rows32[6:8, lane : lane + 128] = before[p * 8 + 6 : p * 8 + 8]
        rows32[6:8, lane + 128 : lane + 256] = before[p * 8 + 2 : p * 8 + 4]
        rows32[8 + ROWS : 9 + ROWS, lane : lane + 128] = after[p * 8 : p * 8 + 1]
        rows32[8 + ROWS : 9 + ROWS, lane + 128 : lane + 256] = after[p * 8 + 4 : p * 8 + 5]
    arrange(other)
    short_transforms(other)
    frames([(mine * 8, 1), (mine * 8 + 7, 1), (other * 8, 8)])
    power([mine * 8, mine * 8 + 7] + [other * 8 + s for s in range(8)], False)

    low_half = lax.broadcasted_iota(jnp.int32, (16, 8, 256), 1) < 4
    left = acc[:, :256].reshape(16, 8, 256)
    right = acc[:, 256:].reshape(16, 8, 256)
    even = jnp.where(low_half, left, pltpu.roll(right, 4, 1))
    odd = jnp.where(low_half, pltpu.roll(left, 4, 1), right)
    for t in range(16):
        blocks[2 * t] = even[t]
        blocks[2 * t + 1] = odd[t]

    for dy, dx, dc in OWNERS:
        to = ys[dy] * 8 + member(dx, dc)
        send(blocks.at[to], landed.at[place], 4, 6, at(ys[dy], z, member(dx, dc)))

    landed[place] = blocks[place]
    arrived(landed.at[pl.ds(0, 31)], recv_sem.at[6])
    for i in range(LINE):
        total = landed[i] + landed[8 + i] + landed[16 + i] + landed[24 + i]
        out[:, i * WIDTH : i * WIDTH + 256] = total[0:4]
        out[:, i * WIDTH + 256 : (i + 1) * WIDTH] = total[4:8]

    @pl.when(mine == 0)
    def _():
        arrived(buf.at[pl.ds(0, 3)], send_sem.at[0])

    @pl.when(mine == 1)
    def _():
        arrived(buf.at[pl.ds(0, 7)], send_sem.at[0])

    @pl.when((z == 0) | (z == 3))
    def _():
        arrived(buf.at[pl.ds(0, 8)], send_sem.at[5])

    arrived(buf.at[pl.ds(0, 28)], send_sem.at[1])
    arrived(buf.at[pl.ds(0, 28)], send_sem.at[2])

    @pl.when((line == 0) & (y > 0))
    def _():
        arrived(buf.at[pl.ds(0, 8)], send_sem.at[3])

    @pl.when((line == 7) & (y < PLANES - 1))
    def _():
        arrived(buf.at[pl.ds(0, 8)], send_sem.at[3])

    arrived(blocks.at[pl.ds(0, 31)], send_sem.at[4])


def body(raw, taper, seg_window):
    channel_table, turn_table, step_table = tables()
    operands = (
        raw, taper.reshape(8, 128), seg_window.reshape(32, 128),
        jnp.asarray(step_table), jnp.asarray(channel_table), jnp.asarray(turn_table),
    )
    vmem = pl.BlockSpec(memory_space=pltpu.VMEM)
    hbm = pl.BlockSpec(memory_space=pltpu.HBM)
    return pl.pallas_call(
        kernel,
        out_shape=jax.ShapeDtypeStruct((4, NFFT), F32),
        in_specs=[hbm] * 6,
        out_specs=vmem,
        scratch_shapes=[
            pltpu.VMEM((2, 1024), BF16),
            pltpu.VMEM((8, 128), F32),
            pltpu.VMEM((32, 128), F32),
            pltpu.VMEM((2, 16, 128), F32),
            pltpu.VMEM((64, 16, 128), BF16),
            pltpu.VMEM((2, 16, 128), BF16),
            pltpu.VMEM((ROWS + 16, 512), F32),
            pltpu.VMEM((2 * STRIP, CHANNELS), F32),
            pltpu.VMEM((4, 2 * STRIP, 512), BF16),
            pltpu.VMEM((2, 512, WIDTH), BF16),
            pltpu.VMEM((2, PER_SEG, WIDTH), F32),
            pltpu.VMEM((PLANE_SEG, 2 * STRIP, 64), BF16),
            pltpu.VMEM((PLANE_SEG, 64, WIDTH), BF16),
            pltpu.VMEM((STRIP, WIDTH), F32),
            pltpu.VMEM((32, 8, 256), F32),
            pltpu.VMEM((32, 8, 256), F32),
            pltpu.SemaphoreType.DMA((6,)),
            pltpu.SemaphoreType.DMA((6,)),
            pltpu.SemaphoreType.DMA((11,)),
        ],
        compiler_params=pltpu.CompilerParams(
            collective_id=0, has_side_effects=True, vmem_limit_bytes=48 * 1024 * 1024
        ),
    )(*(pltpu.with_memory_space_constraint(x, pltpu.HBM) for x in operands))


def solution(mesh):
    placed = (P(None, ("tm", "grp")), P(), P())
    return jax.shard_map(
        body, mesh=mesh, in_specs=placed, out_specs=P(("tm", "grp"), None), check_vma=False
    )
```

```python
import math

import jax
import jax.numpy as jnp
import numpy as np
from jax import lax
from jax.experimental import pallas as pl
from jax.experimental.pallas import tpu as pltpu
from jax.sharding import PartitionSpec as P

MESH = pl.DeviceIdType.MESH
F32 = jnp.float32
BF16 = jnp.bfloat16

CHANNELS = 1024
NFFT = 4096
STRIDE = 256
PER_SEG = NFFT // STRIDE
SEG = 64
PLANES, DEPTH, LINE = 4, 8, 8
PLANE_SEG = SEG // PLANES
ROWS = PLANE_SEG * PER_SEG
HALF_ROWS = ROWS // 2
STRIP = PLANES * LINE * 4
WIDTH = NFFT // LINE
HOPS = (0, 1, 2, 1)
MEMBERS = sorted(((dx, dc) for dx in range(4) for dc in range(2) if dx or dc), key=lambda m: -HOPS[m[0]])
OWNERS = sorted(
    ((dy, dx, dc) for dy in range(4) for dx in range(4) for dc in range(2) if dy or dx or dc),
    key=lambda m: -(HOPS[m[0]] + HOPS[m[1]]),
)


def tables():
    z = np.arange(DEPTH)[:, None, None]
    row = np.arange(STRIP)[None, :, None]
    channel = (row // 32) * 256 + z * 32 + row % 32
    phase = (channel * np.arange(CHANNELS)[None, None, :]) % CHANNELS
    angle = (np.float32(2.0 * math.pi / CHANNELS) * phase.astype(np.float32)).astype(np.float64)
    channel_table = np.concatenate([np.cos(angle), np.sin(angle)], 1).astype(np.float32)
    q = np.arange(LINE)[:, None, None] * WIDTH + np.arange(WIDTH)[None, None, :]
    turn = 2.0 * np.pi / NFFT * ((q * np.arange(STRIDE)[None, :, None]) % NFFT)
    full = np.concatenate([np.cos(turn), -np.sin(turn)], 1)
    high = full.astype(jnp.bfloat16)
    low = (full - high.astype(np.float64)).astype(jnp.bfloat16)
    turn_table = np.stack([high, low], 1)
    j = np.arange(PER_SEG)[:, None]
    step = 2.0 * np.pi / PER_SEG * ((j * np.arange(WIDTH)[None, :]) % PER_SEG)
    step_table = np.stack([np.cos(step), np.sin(step)]).astype(np.float32)
    return channel_table, turn_table, step_table


def kernel(
    raw_hbm, taper_hbm, window_hbm, step_hbm, channel_hbm, turn_hbm, out,
    raw, taper, window, tile32, buf, halo, rows32, coef32, coef, turn, step, lhs, rhs, acc, blocks, landed,
    local_sem, send_sem, recv_sem,
):
    tm, grp = lax.axis_index("tm"), lax.axis_index("grp")
    y, z, x_lo = tm // 16, lax.rem(tm // 2, DEPTH), lax.rem(tm, 2)
    x, core = grp // 2 * 2 + x_lo, lax.rem(grp, 2)
    line = x_lo * 4 + grp
    mine, other = z // 4, 1 - z // 4
    zz = lax.rem(z, 4)
    place = y * 8 + line

    xs = [lax.rem(x + d, 4) for d in range(4)]
    ys = [lax.rem(y + d, PLANES) for d in range(PLANES)]
    cores = [core, 1 - core]

    def member(dx, dc):
        return lax.rem(xs[dx], 2) * 4 + xs[dx] // 2 * 2 + cores[dc]

    def at(plane, depth, member):
        return ((plane * DEPTH + depth) * 2 + member // 4, lax.rem(member, 4))

    def send(src, dst, send_at, recv_at, to):
        pltpu.make_async_remote_copy(
            src, dst, send_sem.at[send_at], recv_sem.at[recv_at],
            device_id=to, device_id_type=MESH,
        ).start()

    def arrived(ref, sem):
        pltpu.make_async_copy(ref, ref, sem).wait()

    loads = [
        pltpu.make_async_copy(raw_hbm, raw, local_sem.at[0]),
        pltpu.make_async_copy(taper_hbm, taper, local_sem.at[1]),
        pltpu.make_async_copy(channel_hbm.at[z], coef32, local_sem.at[2]),
        pltpu.make_async_copy(window_hbm, window, local_sem.at[3]),
        pltpu.make_async_copy(step_hbm, step, local_sem.at[4]),
        pltpu.make_async_copy(turn_hbm.at[line], turn, local_sem.at[5]),
    ]
    loads[0].start()

    barrier = pltpu.get_barrier_semaphore()

    def greet(to):
        pl.semaphore_signal(barrier, inc=1, device_id=to, device_id_type=MESH)

    @pl.when(mine == 0)
    def _():
        for i in range(4):
            greet(at(y, 4 + i, line))

    for i in range(1, 4):
        greet(at(y, mine * 4 + lax.rem(zz + i, 4), line))

    for dx, dc in MEMBERS:
        greet(at(y, z, member(dx, dc)))
    for i in range(1, PLANES):
        greet(at(ys[i], z, line))

    @pl.when((y > 0) & (line < 7))
    def _():
        greet(at(y - 1, z, 7))

    @pl.when((y < PLANES - 1) & (line > 0))
    def _():
        greet(at(y + 1, z, 0))

    loads[0].wait()
    pair = raw[...].astype(F32)
    for part in range(2):
        for chunk in range(8):
            odd, frame = chunk % 2, chunk // 2
            value = pair[part : part + 1, chunk * 128 : (chunk + 1) * 128]
            tile32[0, part * 8 + odd * 4 + frame, :] = value[0]
            tile32[1, part * 8 + (1 - odd) * 4 + frame, :] = value[0]
    own = (mine * 8 + line) * 4 + zz
    buf[own] = jnp.where(core == 0, tile32[0], tile32[1]).astype(BF16)

    @pl.when(y == 0)
    def _():
        halo[0] = jnp.zeros((16, 128), BF16)

    @pl.when(y == PLANES - 1)
    def _():
        halo[1] = jnp.zeros((16, 128), BF16)

    sends_ends = ((line == 0) & (y > 0)) | ((line == 7) & (y < PLANES - 1))
    pl.semaphore_wait(barrier, 13 + 4 * mine + 7 * sends_ends.astype(jnp.int32))

    def along_x(part, send_at, recv_at):
        block = buf.at[pl.ds((part * 8 + line) * 4, 4)]
        for dx, dc in MEMBERS:
            send(block, block, send_at, recv_at, at(y, z, member(dx, dc)))

    def ends(part):
        @pl.when((part == 0) & (line == 0) & (y > 0))
        def _():
            for i in range(8):
                send(buf.at[0], halo.at[1], 3, 5, at(y - 1, z, i))

        @pl.when((part == 1) & (line == 7) & (y < PLANES - 1))
        def _():
            for i in range(8):
                send(buf.at[63], halo.at[0], 3, 4, at(y + 1, z, i))

    @pl.when(mine == 1)
    def _():
        for i in range(4):
            send(buf.at[own], buf.at[own], 0, 7 + zz, at(y, i, line))

    for i in range(1, 4):
        send(buf.at[own], buf.at[own], 0, 0, at(y, mine * 4 + lax.rem(zz + i, 4), line))

    for load in loads[1:]:
        load.start()

    loads[1].wait()
    loads[2].wait()
    for a in range(4):
        for h in range(2):
            i = a * 2 + h
            weight = taper[i : i + 1, :] / math.sqrt(CHANNELS)
            cosine = (weight * coef32[:STRIP, i * 128 : (i + 1) * 128]).astype(BF16)
            sine = (weight * coef32[STRIP:, i * 128 : (i + 1) * 128]).astype(BF16)
            coef[a, :STRIP, h * 128 : (h + 1) * 128] = cosine
            coef[a, STRIP:, h * 128 : (h + 1) * 128] = -sine
            coef[a, :STRIP, 256 + h * 128 : 256 + (h + 1) * 128] = sine
            coef[a, STRIP:, 256 + h * 128 : 256 + (h + 1) * 128] = cosine

    arrived(buf.at[pl.ds(0, 3)], recv_sem.at[0])
    along_x(mine, 1, 2)
    ends(mine)
    low_rows = lax.broadcasted_iota(jnp.int32, (4, 8, 128), 1) < 4

    def arrange(part):
        start = pl.multiple_of(8 + part * HALF_ROWS, 8)
        for p in range(2):
            evens, odds = [], []
            for i in range(4):
                first = buf[pl.ds((part * 8 + 2 * i) * 4, 4)].astype(F32)[:, p * 8 : p * 8 + 8]
                second = buf[pl.ds((part * 8 + 2 * i + 1) * 4, 4)].astype(F32)[:, p * 8 : p * 8 + 8]
                evens.append(jnp.where(low_rows, first, second))
                odds.append(pltpu.roll(jnp.where(low_rows, second, first), 4, 1))
            for h, pieces in enumerate((evens, odds)):
                at_lane = p * 256 + h * 128
                rows32[pl.ds(start, HALF_ROWS), at_lane : at_lane + 128] = jnp.stack(pieces, 1).reshape(HALF_ROWS, 128)

    def short_transforms(part):
        start = pl.multiple_of(8 + part * HALF_ROWS, 8)
        parts = []
        for p in range(2):
            value = rows32[pl.ds(start, HALF_ROWS), p * 256 : (p + 1) * 256].reshape(8, PER_SEG, STRIDE)
            parts.append((value * wins[None]).reshape(HALF_ROWS, STRIDE))
        samples = jnp.concatenate(
            [jnp.concatenate(parts, 1), jnp.concatenate([-parts[1], parts[0]], 1)], 0
        )
        high = samples.astype(BF16)
        low = (samples - high.astype(F32)).astype(BF16)
        turned = (
            jnp.dot(high, turn[0], preferred_element_type=F32)
            + jnp.dot(high, turn[1], preferred_element_type=F32)
            + jnp.dot(low, turn[0], preferred_element_type=F32)
        )
        g_re = turned[:HALF_ROWS].reshape(8, PER_SEG, WIDTH)
        g_im = turned[HALF_ROWS:].reshape(8, PER_SEG, WIDTH)
        cos_step, sin_step = step[0][None], step[1][None]
        for i, value in enumerate((g_re * cos_step + g_im * sin_step, g_im * cos_step - g_re * sin_step)):
            top = value.astype(BF16)
            rhs[pl.ds(part * 8, 8), i * 16 : i * 16 + 16, :] = top
            rhs[pl.ds(part * 8, 8), 32 + i * 16 : 48 + i * 16, :] = (value - top.astype(F32)).astype(BF16)

    def frames(runs):
        pieces = []
        for first, count in runs:
            start = pl.multiple_of(first * PER_SEG, 16)
            pieces.append(rows32[pl.ds(start, (count + 1) * PER_SEG), :].astype(BF16))
        rows = jnp.concatenate(pieces, 0)
        total = None
        for a in range(4):
            term = lax.dot_general(rows, coef[a], (((1,), (1,)), ((), ())), preferred_element_type=F32)
            taken, row = [], 6 + a
            for first, count in runs:
                taken.append(term[row : row + count * PER_SEG])
                row += (count + 1) * PER_SEG
            term = jnp.concatenate(taken, 0)
            total = term if total is None else total + term
        rounded = total.astype(BF16).astype(F32)
        swapped = jnp.concatenate([-rounded[:, STRIP:], rounded[:, :STRIP]], 1)
        row = 0
        for first, count in runs:
            for s in range(count):
                pair = jnp.concatenate([rounded[row : row + PER_SEG], swapped[row : row + PER_SEG]], 0)
                lhs[first + s] = jnp.concatenate([pair, pair], 0).T.astype(BF16)
                row += PER_SEG

    def power(segments, first):
        for n in range(2):
            lanes = slice(n * 256, (n + 1) * 256)
            total = None if first else acc[:, lanes]
            for s in segments:
                e = jnp.dot(lhs[s], rhs[s][:, lanes], preferred_element_type=F32)
                term = e[:STRIP] * e[:STRIP] + e[STRIP:] * e[STRIP:]
                total = term if total is None else total + term
            acc[:, lanes] = total

    def late_tile(i):
        arrived(buf.at[0], recv_sem.at[7 + i])

    def early_block(i):
        block = buf.at[pl.ds(line * 4, 4)]
        send(block, block, 5, 1, at(y, 4 + i, line))

    @pl.when(z == 0)
    def _():
        for i in (3, 2):
            late_tile(i)
            early_block(i)
        late_tile(1)
        late_tile(0)

    @pl.when(z == 3)
    def _():
        for i in (0, 1):
            late_tile(i)
            early_block(i)
        late_tile(2)
        late_tile(3)

    @pl.when((z == 1) | (z == 2))
    def _():
        for i in range(4):
            late_tile(i)

    @pl.when(mine == 1)
    def _():
        arrived(buf.at[pl.ds(0, 4)], recv_sem.at[1])

    along_x(other, 2, 3)
    ends(other)

    for load in loads[3:]:
        load.wait()

    wins = jnp.concatenate(
        [window[pl.ds(0, PER_SEG, stride=2), :], window[pl.ds(1, PER_SEG, stride=2), :]], 1
    ) * (1.0 / 512.0)
    arrived(buf.at[pl.ds(0, 28)], recv_sem.at[2])
    arrange(mine)
    short_transforms(mine)
    frames([(mine * 8 + 1, 6)])
    power([mine * 8 + s for s in range(1, 7)], True)

    arrived(buf.at[pl.ds(0, 28)], recv_sem.at[3])

    @pl.when(y > 0)
    def _():
        arrived(halo.at[0], recv_sem.at[4])

    @pl.when(y < PLANES - 1)
    def _():
        arrived(halo.at[1], recv_sem.at[5])

    before, after = halo[0].astype(F32), halo[1].astype(F32)
    for p in range(2):
        lane = p * 256
        rows32[6:8, lane : lane + 128] = before[p * 8 + 6 : p * 8 + 8]
        rows32[6:8, lane + 128 : lane + 256] = before[p * 8 + 2 : p * 8 + 4]
        rows32[8 + ROWS : 9 + ROWS, lane : lane + 128] = after[p * 8 : p * 8 + 1]
        rows32[8 + ROWS : 9 + ROWS, lane + 128 : lane + 256] = after[p * 8 + 4 : p * 8 + 5]
    arrange(other)
    short_transforms(other)
    frames([(mine * 8, 1), (mine * 8 + 7, 1), (other * 8, 8)])
    power([mine * 8, mine * 8 + 7] + [other * 8 + s for s in range(8)], False)

    low_half = lax.broadcasted_iota(jnp.int32, (16, 8, 256), 1) < 4
    left = acc[:, :256].reshape(16, 8, 256)
    right = acc[:, 256:].reshape(16, 8, 256)
    even = jnp.where(low_half, left, pltpu.roll(right, 4, 1))
    odd = jnp.where(low_half, pltpu.roll(left, 4, 1), right)
    for t in range(16):
        blocks[2 * t] = even[t]
        blocks[2 * t + 1] = odd[t]

    for dy, dx, dc in OWNERS:
        to = ys[dy] * 8 + member(dx, dc)
        send(blocks.at[to], landed.at[place], 4, 6, at(ys[dy], z, member(dx, dc)))

    landed[place] = blocks[place]
    arrived(landed.at[pl.ds(0, 31)], recv_sem.at[6])
    for i in range(LINE):
        total = landed[i] + landed[8 + i] + landed[16 + i] + landed[24 + i]
        out[:, i * WIDTH : i * WIDTH + 256] = total[0:4]
        out[:, i * WIDTH + 256 : (i + 1) * WIDTH] = total[4:8]

    @pl.when(mine == 0)
    def _():
        arrived(buf.at[pl.ds(0, 3)], send_sem.at[0])

    @pl.when(mine == 1)
    def _():
        arrived(buf.at[pl.ds(0, 7)], send_sem.at[0])

    @pl.when((z == 0) | (z == 3))
    def _():
        arrived(buf.at[pl.ds(0, 8)], send_sem.at[5])

    arrived(buf.at[pl.ds(0, 28)], send_sem.at[1])
    arrived(buf.at[pl.ds(0, 28)], send_sem.at[2])

    @pl.when((line == 0) & (y > 0))
    def _():
        arrived(buf.at[pl.ds(0, 8)], send_sem.at[3])

    @pl.when((line == 7) & (y < PLANES - 1))
    def _():
        arrived(buf.at[pl.ds(0, 8)], send_sem.at[3])

    arrived(blocks.at[pl.ds(0, 31)], send_sem.at[4])


def body(raw, taper, seg_window):
    channel_table, turn_table, step_table = tables()
    operands = (
        raw, taper.reshape(8, 128), seg_window.reshape(32, 128),
        jnp.asarray(step_table), jnp.asarray(channel_table), jnp.asarray(turn_table),
    )
    vmem = pl.BlockSpec(memory_space=pltpu.VMEM)
    hbm = pl.BlockSpec(memory_space=pltpu.HBM)
    return pl.pallas_call(
        kernel,
        out_shape=jax.ShapeDtypeStruct((4, NFFT), F32),
        in_specs=[hbm] * 6,
        out_specs=vmem,
        scratch_shapes=[
            pltpu.VMEM((2, 1024), BF16),
            pltpu.VMEM((8, 128), F32),
            pltpu.VMEM((32, 128), F32),
            pltpu.VMEM((2, 16, 128), F32),
            pltpu.VMEM((64, 16, 128), BF16),
            pltpu.VMEM((2, 16, 128), BF16),
            pltpu.VMEM((ROWS + 16, 512), F32),
            pltpu.VMEM((2 * STRIP, CHANNELS), F32),
            pltpu.VMEM((4, 2 * STRIP, 512), BF16),
            pltpu.VMEM((2, 512, WIDTH), BF16),
            pltpu.VMEM((2, PER_SEG, WIDTH), F32),
            pltpu.VMEM((PLANE_SEG, 2 * STRIP, 64), BF16),
            pltpu.VMEM((PLANE_SEG, 64, WIDTH), BF16),
            pltpu.VMEM((STRIP, WIDTH), F32),
            pltpu.VMEM((32, 8, 256), F32),
            pltpu.VMEM((32, 8, 256), F32),
            pltpu.SemaphoreType.DMA((6,)),
            pltpu.SemaphoreType.DMA((6,)),
            pltpu.SemaphoreType.DMA((11,)),
        ],
        compiler_params=pltpu.CompilerParams(
            collective_id=0, has_side_effects=True, vmem_limit_bytes=48 * 1024 * 1024
        ),
    )(*(pltpu.with_memory_space_constraint(x, pltpu.HBM) for x in operands))


def solution(mesh):
    placed = (P(None, ("tm", "grp")), P(), P())
    return jax.shard_map(
        body, mesh=mesh, in_specs=placed, out_specs=P(("tm", "grp"), None), check_vma=False
    )
```

```python
import math

import jax
import jax.numpy as jnp
import numpy as np
from jax import lax
from jax.experimental import pallas as pl
from jax.experimental.pallas import tpu as pltpu
from jax.sharding import PartitionSpec as P

MESH = pl.DeviceIdType.MESH
F32 = jnp.float32
BF16 = jnp.bfloat16

CHANNELS = 1024
NFFT = 4096
STRIDE = 256
PER_SEG = NFFT // STRIDE
SEG = 64
PLANES, DEPTH, LINE = 4, 8, 8
PLANE_SEG = SEG // PLANES
ROWS = PLANE_SEG * PER_SEG
HALF_ROWS = ROWS // 2
STRIP = PLANES * LINE * 4
WIDTH = NFFT // LINE
HOPS = (0, 1, 2, 1)
MEMBERS = sorted(((dx, dc) for dx in range(4) for dc in range(2) if dx or dc), key=lambda m: -HOPS[m[0]])
OWNERS = sorted(
    ((dy, dx, dc) for dy in range(4) for dx in range(4) for dc in range(2) if dy or dx or dc),
    key=lambda m: -(HOPS[m[0]] + HOPS[m[1]]),
)


def tables():
    z = np.arange(DEPTH)[:, None, None]
    row = np.arange(STRIP)[None, :, None]
    channel = (row // 32) * 256 + z * 32 + row % 32
    phase = (channel * np.arange(CHANNELS)[None, None, :]) % CHANNELS
    angle = (np.float32(2.0 * math.pi / CHANNELS) * phase.astype(np.float32)).astype(np.float64)
    channel_table = np.concatenate([np.cos(angle), np.sin(angle)], 1).astype(np.float32)
    q = np.arange(LINE)[:, None, None] * WIDTH + np.arange(WIDTH)[None, None, :]
    turn = 2.0 * np.pi / NFFT * ((q * np.arange(STRIDE)[None, :, None]) % NFFT)
    full = np.concatenate([np.cos(turn), -np.sin(turn)], 1)
    high = full.astype(jnp.bfloat16)
    low = (full - high.astype(np.float64)).astype(jnp.bfloat16)
    turn_table = np.stack([high, low], 1)
    j = np.arange(PER_SEG)[:, None]
    step = 2.0 * np.pi / PER_SEG * ((j * np.arange(WIDTH)[None, :]) % PER_SEG)
    step_table = np.stack([np.cos(step), np.sin(step)]).astype(np.float32)
    return channel_table, turn_table, step_table


def kernel(
    raw_hbm, taper_hbm, window_hbm, step_hbm, channel_hbm, turn_hbm, out,
    raw, taper, window, tile32, buf, halo, rows32, coef32, coef, turn, step, lhs, rhs, acc, blocks, landed,
    local_sem, send_sem, recv_sem, known,
):
    tm, grp = lax.axis_index("tm"), lax.axis_index("grp")
    y, z, x_lo = tm // 16, lax.rem(tm // 2, DEPTH), lax.rem(tm, 2)
    x, core = grp // 2 * 2 + x_lo, lax.rem(grp, 2)
    line = x_lo * 4 + grp
    mine, other = z // 4, 1 - z // 4
    zz = lax.rem(z, 4)
    place = y * 8 + line

    xs = [lax.rem(x + d, 4) for d in range(4)]
    ys = [lax.rem(y + d, PLANES) for d in range(PLANES)]
    cores = [core, 1 - core]

    def member(dx, dc):
        return lax.rem(xs[dx], 2) * 4 + xs[dx] // 2 * 2 + cores[dc]

    def at(plane, depth, member):
        return ((plane * DEPTH + depth) * 2 + member // 4, lax.rem(member, 4))

    def send(src, dst, send_at, recv_at, to):
        pltpu.make_async_remote_copy(
            src, dst, send_sem.at[send_at], recv_sem.at[recv_at],
            device_id=to, device_id_type=MESH,
        ).start()

    def arrived(ref, sem):
        pltpu.make_async_copy(ref, ref, sem).wait()

    loads = [
        pltpu.make_async_copy(raw_hbm, raw, local_sem.at[0]),
        pltpu.make_async_copy(taper_hbm, taper, local_sem.at[1]),
        pltpu.make_async_copy(channel_hbm.at[z], coef32, local_sem.at[2]),
        pltpu.make_async_copy(window_hbm, window, local_sem.at[3]),
        pltpu.make_async_copy(step_hbm, step, local_sem.at[4]),
        pltpu.make_async_copy(turn_hbm.at[line], turn, local_sem.at[5]),
    ]
    loads[0].start()

    barrier = pltpu.get_barrier_semaphore()
    even_core, odd_core = line - core, line - core + 1

    def greet(to):
        pl.semaphore_signal(barrier, inc=1, device_id=to, device_id_type=MESH)

    @pl.when(mine == 0)
    def _():
        for i in range(4):
            greet(at(y, 4 + i, even_core))
        for i in range(1, 4):
            greet(at(y, lax.rem(zz + i, 4), line))
        for dx, dc in MEMBERS:
            greet(at(y, z, member(dx, dc)))
        for i in range(1, PLANES):
            greet(at(ys[i], z, line))

        @pl.when((y > 0) & (line < 7))
        def _():
            greet(at(y - 1, z, 7))

        @pl.when((y < PLANES - 1) & (line > 0))
        def _():
            greet(at(y + 1, z, 0))

    @pl.when(mine == 1)
    def _():
        @pl.when(core == 1)
        def _():
            greet(at(y, z, even_core))

        for i in range(1, 4):
            greet(at(y, 4 + lax.rem(zz + i, 4), odd_core))
        for dx in (2, 1, 3):
            greet(at(y, z, lax.rem(xs[dx], 2) * 4 + xs[dx] // 2 * 2 + 1))
        for i in range(1, PLANES):
            greet(at(ys[i], z, odd_core))

        @pl.when((y > 0) & (line < 6))
        def _():
            greet(at(y - 1, z, 7))

        @pl.when((y < PLANES - 1) & (line > 1))
        def _():
            greet(at(y + 1, z, 1))

    loads[0].wait()
    pair = raw[...].astype(F32)
    for part in range(2):
        for chunk in range(8):
            odd, frame = chunk % 2, chunk // 2
            value = pair[part : part + 1, chunk * 128 : (chunk + 1) * 128]
            tile32[0, part * 8 + odd * 4 + frame, :] = value[0]
            tile32[1, part * 8 + (1 - odd) * 4 + frame, :] = value[0]
    own = (mine * 8 + line) * 4 + zz
    buf[own] = jnp.where(core == 0, tile32[0], tile32[1]).astype(BF16)

    @pl.when(y == 0)
    def _():
        halo[0] = jnp.zeros((16, 128), BF16)

    @pl.when(y == PLANES - 1)
    def _():
        halo[1] = jnp.zeros((16, 128), BF16)

    partner = at(y, z, member(0, 1))
    last, first = (line == 7) & (y < PLANES - 1), y > 0

    @pl.when(mine == 0)
    def _():
        pl.semaphore_wait(barrier, 13 + 7 * (last | ((line == 0) & first)).astype(jnp.int32))

    @pl.when((mine == 1) & (core == 0))
    def _():
        pl.semaphore_wait(barrier, 9)
        pl.semaphore_signal(known.at[0], inc=1, device_id=partner, device_id_type=MESH)

    @pl.when((mine == 1) & (core == 1))
    def _():
        pl.semaphore_wait(known.at[0], 1)

    @pl.when(mine == 1)
    def _():
        for i in range(4):
            send(buf.at[own], buf.at[own], 0, 7 + zz, at(y, i, line))

    @pl.when((mine == 1) & (core == 1))
    def _():
        pl.semaphore_wait(barrier, 18 + 6 * (last | ((line == 1) & first)).astype(jnp.int32))
        pl.semaphore_signal(known.at[1], inc=1, device_id=partner, device_id_type=MESH)

    @pl.when((mine == 1) & (core == 0))
    def _():
        pl.semaphore_wait(known.at[1], 1)

    def along_x(part, send_at, recv_at):
        block = buf.at[pl.ds((part * 8 + line) * 4, 4)]
        for dx, dc in MEMBERS:
            send(block, block, send_at, recv_at, at(y, z, member(dx, dc)))

    def ends(part):
        @pl.when((part == 0) & (line == 0) & (y > 0))
        def _():
            for i in range(8):
                send(buf.at[0], halo.at[1], 3, 5, at(y - 1, z, i))

        @pl.when((part == 1) & (line == 7) & (y < PLANES - 1))
        def _():
            for i in range(8):
                send(buf.at[63], halo.at[0], 3, 4, at(y + 1, z, i))

    for i in range(1, 4):
        send(buf.at[own], buf.at[own], 0, 0, at(y, mine * 4 + lax.rem(zz + i, 4), line))

    for load in loads[1:]:
        load.start()

    loads[1].wait()
    loads[2].wait()
    for a in range(4):
        for h in range(2):
            i = a * 2 + h
            weight = taper[i : i + 1, :] / math.sqrt(CHANNELS)
            cosine = (weight * coef32[:STRIP, i * 128 : (i + 1) * 128]).astype(BF16)
            sine = (weight * coef32[STRIP:, i * 128 : (i + 1) * 128]).astype(BF16)
            coef[a, :STRIP, h * 128 : (h + 1) * 128] = cosine
            coef[a, STRIP:, h * 128 : (h + 1) * 128] = -sine
            coef[a, :STRIP, 256 + h * 128 : 256 + (h + 1) * 128] = sine
            coef[a, STRIP:, 256 + h * 128 : 256 + (h + 1) * 128] = cosine

    arrived(buf.at[pl.ds(0, 3)], recv_sem.at[0])
    along_x(mine, 1, 2)
    ends(mine)
    low_rows = lax.broadcasted_iota(jnp.int32, (4, 8, 128), 1) < 4

    def arrange(part):
        start = pl.multiple_of(8 + part * HALF_ROWS, 8)
        for p in range(2):
            evens, odds = [], []
            for i in range(4):
                first = buf[pl.ds((part * 8 + 2 * i) * 4, 4)].astype(F32)[:, p * 8 : p * 8 + 8]
                second = buf[pl.ds((part * 8 + 2 * i + 1) * 4, 4)].astype(F32)[:, p * 8 : p * 8 + 8]
                evens.append(jnp.where(low_rows, first, second))
                odds.append(pltpu.roll(jnp.where(low_rows, second, first), 4, 1))
            for h, pieces in enumerate((evens, odds)):
                at_lane = p * 256 + h * 128
                rows32[pl.ds(start, HALF_ROWS), at_lane : at_lane + 128] = jnp.stack(pieces, 1).reshape(HALF_ROWS, 128)

    def short_transforms(part):
        start = pl.multiple_of(8 + part * HALF_ROWS, 8)
        parts = []
        for p in range(2):
            value = rows32[pl.ds(start, HALF_ROWS), p * 256 : (p + 1) * 256].reshape(8, PER_SEG, STRIDE)
            parts.append((value * wins[None]).reshape(HALF_ROWS, STRIDE))
        samples = jnp.concatenate(
            [jnp.concatenate(parts, 1), jnp.concatenate([-parts[1], parts[0]], 1)], 0
        )
        high = samples.astype(BF16)
        low = (samples - high.astype(F32)).astype(BF16)
        turned = (
            jnp.dot(high, turn[0], preferred_element_type=F32)
            + jnp.dot(high, turn[1], preferred_element_type=F32)
            + jnp.dot(low, turn[0], preferred_element_type=F32)
        )
        g_re = turned[:HALF_ROWS].reshape(8, PER_SEG, WIDTH)
        g_im = turned[HALF_ROWS:].reshape(8, PER_SEG, WIDTH)
        cos_step, sin_step = step[0][None], step[1][None]
        for i, value in enumerate((g_re * cos_step + g_im * sin_step, g_im * cos_step - g_re * sin_step)):
            top = value.astype(BF16)
            rhs[pl.ds(part * 8, 8), i * 16 : i * 16 + 16, :] = top
            rhs[pl.ds(part * 8, 8), 32 + i * 16 : 48 + i * 16, :] = (value - top.astype(F32)).astype(BF16)

    def frames(runs):
        pieces = []
        for first, count in runs:
            start = pl.multiple_of(first * PER_SEG, 16)
            pieces.append(rows32[pl.ds(start, (count + 1) * PER_SEG), :].astype(BF16))
        rows = jnp.concatenate(pieces, 0)
        total = None
        for a in range(4):
            term = lax.dot_general(rows, coef[a], (((1,), (1,)), ((), ())), preferred_element_type=F32)
            taken, row = [], 6 + a
            for first, count in runs:
                taken.append(term[row : row + count * PER_SEG])
                row += (count + 1) * PER_SEG
            term = jnp.concatenate(taken, 0)
            total = term if total is None else total + term
        rounded = total.astype(BF16).astype(F32)
        swapped = jnp.concatenate([-rounded[:, STRIP:], rounded[:, :STRIP]], 1)
        row = 0
        for first, count in runs:
            for s in range(count):
                pair = jnp.concatenate([rounded[row : row + PER_SEG], swapped[row : row + PER_SEG]], 0)
                lhs[first + s] = jnp.concatenate([pair, pair], 0).T.astype(BF16)
                row += PER_SEG

    def power(segments, first):
        for n in range(2):
            lanes = slice(n * 256, (n + 1) * 256)
            total = None if first else acc[:, lanes]
            for s in segments:
                e = jnp.dot(lhs[s], rhs[s][:, lanes], preferred_element_type=F32)
                term = e[:STRIP] * e[:STRIP] + e[STRIP:] * e[STRIP:]
                total = term if total is None else total + term
            acc[:, lanes] = total

    def late_tile(i):
        arrived(buf.at[0], recv_sem.at[7 + i])

    def early_block(i):
        block = buf.at[pl.ds(line * 4, 4)]
        send(block, block, 5, 1, at(y, 4 + i, line))

    @pl.when(z == 0)
    def _():
        for i in (3, 2):
            late_tile(i)
            early_block(i)
        late_tile(1)
        late_tile(0)

    @pl.when(z == 3)
    def _():
        for i in (0, 1):
            late_tile(i)
            early_block(i)
        late_tile(2)
        late_tile(3)

    @pl.when((z == 1) | (z == 2))
    def _():
        for i in range(4):
            late_tile(i)

    @pl.when(mine == 1)
    def _():
        arrived(buf.at[pl.ds(0, 4)], recv_sem.at[1])

    along_x(other, 2, 3)
    ends(other)

    for load in loads[3:]:
        load.wait()

    wins = jnp.concatenate(
        [window[pl.ds(0, PER_SEG, stride=2), :], window[pl.ds(1, PER_SEG, stride=2), :]], 1
    ) * (1.0 / 512.0)
    arrived(buf.at[pl.ds(0, 28)], recv_sem.at[2])
    arrange(mine)
    short_transforms(mine)
    frames([(mine * 8 + 1, 6)])
    power([mine * 8 + s for s in range(1, 7)], True)

    arrived(buf.at[pl.ds(0, 28)], recv_sem.at[3])

    @pl.when(y > 0)
    def _():
        arrived(halo.at[0], recv_sem.at[4])

    @pl.when(y < PLANES - 1)
    def _():
        arrived(halo.at[1], recv_sem.at[5])

    before, after = halo[0].astype(F32), halo[1].astype(F32)
    for p in range(2):
        lane = p * 256
        rows32[6:8, lane : lane + 128] = before[p * 8 + 6 : p * 8 + 8]
        rows32[6:8, lane + 128 : lane + 256] = before[p * 8 + 2 : p * 8 + 4]
        rows32[8 + ROWS : 9 + ROWS, lane : lane + 128] = after[p * 8 : p * 8 + 1]
        rows32[8 + ROWS : 9 + ROWS, lane + 128 : lane + 256] = after[p * 8 + 4 : p * 8 + 5]
    arrange(other)
    short_transforms(other)
    frames([(mine * 8, 1), (mine * 8 + 7, 1), (other * 8, 8)])
    power([mine * 8, mine * 8 + 7] + [other * 8 + s for s in range(8)], False)

    low_half = lax.broadcasted_iota(jnp.int32, (16, 8, 256), 1) < 4
    left = acc[:, :256].reshape(16, 8, 256)
    right = acc[:, 256:].reshape(16, 8, 256)
    even = jnp.where(low_half, left, pltpu.roll(right, 4, 1))
    odd = jnp.where(low_half, pltpu.roll(left, 4, 1), right)
    for t in range(16):
        blocks[2 * t] = even[t]
        blocks[2 * t + 1] = odd[t]

    for dy, dx, dc in OWNERS:
        to = ys[dy] * 8 + member(dx, dc)
        send(blocks.at[to], landed.at[place], 4, 6, at(ys[dy], z, member(dx, dc)))

    landed[place] = blocks[place]
    arrived(landed.at[pl.ds(0, 31)], recv_sem.at[6])
    for i in range(LINE):
        total = landed[i] + landed[8 + i] + landed[16 + i] + landed[24 + i]
        out[:, i * WIDTH : i * WIDTH + 256] = total[0:4]
        out[:, i * WIDTH + 256 : (i + 1) * WIDTH] = total[4:8]

    @pl.when(mine == 0)
    def _():
        arrived(buf.at[pl.ds(0, 3)], send_sem.at[0])

    @pl.when(mine == 1)
    def _():
        arrived(buf.at[pl.ds(0, 7)], send_sem.at[0])

    @pl.when((z == 0) | (z == 3))
    def _():
        arrived(buf.at[pl.ds(0, 8)], send_sem.at[5])

    arrived(buf.at[pl.ds(0, 28)], send_sem.at[1])
    arrived(buf.at[pl.ds(0, 28)], send_sem.at[2])

    @pl.when((line == 0) & (y > 0))
    def _():
        arrived(buf.at[pl.ds(0, 8)], send_sem.at[3])

    @pl.when((line == 7) & (y < PLANES - 1))
    def _():
        arrived(buf.at[pl.ds(0, 8)], send_sem.at[3])

    arrived(blocks.at[pl.ds(0, 31)], send_sem.at[4])


def body(raw, taper, seg_window):
    channel_table, turn_table, step_table = tables()
    operands = (
        raw, taper.reshape(8, 128), seg_window.reshape(32, 128),
        jnp.asarray(step_table), jnp.asarray(channel_table), jnp.asarray(turn_table),
    )
    vmem = pl.BlockSpec(memory_space=pltpu.VMEM)
    hbm = pl.BlockSpec(memory_space=pltpu.HBM)
    return pl.pallas_call(
        kernel,
        out_shape=jax.ShapeDtypeStruct((4, NFFT), F32),
        in_specs=[hbm] * 6,
        out_specs=vmem,
        scratch_shapes=[
            pltpu.VMEM((2, 1024), BF16),
            pltpu.VMEM((8, 128), F32),
            pltpu.VMEM((32, 128), F32),
            pltpu.VMEM((2, 16, 128), F32),
            pltpu.VMEM((64, 16, 128), BF16),
            pltpu.VMEM((2, 16, 128), BF16),
            pltpu.VMEM((ROWS + 16, 512), F32),
            pltpu.VMEM((2 * STRIP, CHANNELS), F32),
            pltpu.VMEM((4, 2 * STRIP, 512), BF16),
            pltpu.VMEM((2, 512, WIDTH), BF16),
            pltpu.VMEM((2, PER_SEG, WIDTH), F32),
            pltpu.VMEM((PLANE_SEG, 2 * STRIP, 64), BF16),
            pltpu.VMEM((PLANE_SEG, 64, WIDTH), BF16),
            pltpu.VMEM((STRIP, WIDTH), F32),
            pltpu.VMEM((32, 8, 256), F32),
            pltpu.VMEM((32, 8, 256), F32),
            pltpu.SemaphoreType.DMA((6,)),
            pltpu.SemaphoreType.DMA((6,)),
            pltpu.SemaphoreType.DMA((11,)),
            pltpu.SemaphoreType.REGULAR((2,)),
        ],
        compiler_params=pltpu.CompilerParams(
            collective_id=0, has_side_effects=True, vmem_limit_bytes=48 * 1024 * 1024
        ),
    )(*(pltpu.with_memory_space_constraint(x, pltpu.HBM) for x in operands))


def solution(mesh):
    placed = (P(None, ("tm", "grp")), P(), P())
    return jax.shard_map(
        body, mesh=mesh, in_specs=placed, out_specs=P(("tm", "grp"), None), check_vma=False
    )
```

```python
import math

import jax
import jax.numpy as jnp
import numpy as np
from jax import lax
from jax.experimental import pallas as pl
from jax.experimental.pallas import tpu as pltpu
from jax.sharding import PartitionSpec as P

MESH = pl.DeviceIdType.MESH
F32 = jnp.float32
BF16 = jnp.bfloat16

CHANNELS = 1024
NFFT = 4096
STRIDE = 256
PER_SEG = NFFT // STRIDE
SEG = 64
PLANES, DEPTH, LINE = 4, 8, 8
PLANE_SEG = SEG // PLANES
ROWS = PLANE_SEG * PER_SEG
HALF_ROWS = ROWS // 2
STRIP = PLANES * LINE * 4
WIDTH = NFFT // LINE
HOPS = (0, 1, 2, 1)
MEMBERS = sorted(((dx, dc) for dx in range(4) for dc in range(2) if dx or dc), key=lambda m: -HOPS[m[0]])
FIRST = 1
OWNERS = sorted(
    ((dy, dx, dc) for dy in range(4) for dx in range(4) for dc in range(2) if dy or dx or dc),
    key=lambda m: -(HOPS[m[0]] + HOPS[m[1]]),
)


def tables():
    z = np.arange(DEPTH)[:, None, None]
    row = np.arange(STRIP)[None, :, None]
    channel = (row // 32) * 256 + z * 32 + row % 32
    phase = (channel * np.arange(CHANNELS)[None, None, :]) % CHANNELS
    angle = (np.float32(2.0 * math.pi / CHANNELS) * phase.astype(np.float32)).astype(np.float64)
    channel_table = np.concatenate([np.cos(angle), np.sin(angle)], 1).astype(np.float32)
    q = np.arange(LINE)[:, None, None] * WIDTH + np.arange(WIDTH)[None, None, :]
    turn = 2.0 * np.pi / NFFT * ((q * np.arange(STRIDE)[None, :, None]) % NFFT)
    full = np.concatenate([np.cos(turn), -np.sin(turn)], 1)
    high = full.astype(jnp.bfloat16)
    low = (full - high.astype(np.float64)).astype(jnp.bfloat16)
    turn_table = np.stack([high, low], 1)
    j = np.arange(PER_SEG)[:, None]
    step = 2.0 * np.pi / PER_SEG * ((j * np.arange(WIDTH)[None, :]) % PER_SEG)
    step_table = np.stack([np.cos(step), np.sin(step)]).astype(np.float32)
    return channel_table, turn_table, step_table


def kernel(
    raw_hbm, taper_hbm, window_hbm, step_hbm, channel_hbm, turn_hbm, out,
    raw, taper, window, tile32, buf, halo, rows32, coef32, coef, turn, step, lhs, rhs, acc, blocks, landed,
    local_sem, send_sem, recv_sem, known,
):
    tm, grp = lax.axis_index("tm"), lax.axis_index("grp")
    y, z, x_lo = tm // 16, lax.rem(tm // 2, DEPTH), lax.rem(tm, 2)
    x, core = grp // 2 * 2 + x_lo, lax.rem(grp, 2)
    line = x_lo * 4 + grp
    mine, other = z // 4, 1 - z // 4
    zz = lax.rem(z, 4)
    place = y * 8 + line

    xs = [lax.rem(x + d, 4) for d in range(4)]
    ys = [lax.rem(y + d, PLANES) for d in range(PLANES)]
    cores = [core, 1 - core]

    def member(dx, dc):
        return lax.rem(xs[dx], 2) * 4 + xs[dx] // 2 * 2 + cores[dc]

    def at(plane, depth, member):
        return ((plane * DEPTH + depth) * 2 + member // 4, lax.rem(member, 4))

    def send(src, dst, send_at, recv_at, to):
        pltpu.make_async_remote_copy(
            src, dst, send_sem.at[send_at], recv_sem.at[recv_at],
            device_id=to, device_id_type=MESH,
        ).start()

    def arrived(ref, sem):
        pltpu.make_async_copy(ref, ref, sem).wait()

    loads = [
        pltpu.make_async_copy(raw_hbm, raw, local_sem.at[0]),
        pltpu.make_async_copy(taper_hbm, taper, local_sem.at[1]),
        pltpu.make_async_copy(channel_hbm.at[z], coef32, local_sem.at[2]),
        pltpu.make_async_copy(window_hbm, window, local_sem.at[3]),
        pltpu.make_async_copy(step_hbm, step, local_sem.at[4]),
        pltpu.make_async_copy(turn_hbm.at[line], turn, local_sem.at[5]),
    ]
    loads[0].start()

    barrier = pltpu.get_barrier_semaphore()
    even_core, odd_core = line - core, line - core + 1

    def greet(to):
        pl.semaphore_signal(barrier, inc=1, device_id=to, device_id_type=MESH)

    @pl.when(mine == 0)
    def _():
        for i in range(4):
            greet(at(y, 4 + i, even_core))
        for i in range(1, 4):
            greet(at(y, lax.rem(zz + i, 4), line))
        for dx, dc in MEMBERS:
            greet(at(y, z, member(dx, dc)))
        for i in range(1, PLANES):
            greet(at(ys[i], z, line))

        @pl.when((y > 0) & (line < 7))
        def _():
            greet(at(y - 1, z, 7))

        @pl.when((y < PLANES - 1) & (line > 0))
        def _():
            greet(at(y + 1, z, 0))

    @pl.when(mine == 1)
    def _():
        @pl.when(core == 1)
        def _():
            greet(at(y, z, even_core))

        for i in range(1, 4):
            greet(at(y, 4 + lax.rem(zz + i, 4), odd_core))
        for dx in (2, 1, 3):
            greet(at(y, z, lax.rem(xs[dx], 2) * 4 + xs[dx] // 2 * 2 + 1))
        for i in range(1, PLANES):
            greet(at(ys[i], z, odd_core))

        @pl.when((y > 0) & (line < 6))
        def _():
            greet(at(y - 1, z, 7))

        @pl.when((y < PLANES - 1) & (line > 1))
        def _():
            greet(at(y + 1, z, 1))

    loads[0].wait()
    pair = raw[...].astype(F32)
    for part in range(2):
        for chunk in range(8):
            odd, frame = chunk % 2, chunk // 2
            value = pair[part : part + 1, chunk * 128 : (chunk + 1) * 128]
            tile32[0, part * 8 + odd * 4 + frame, :] = value[0]
            tile32[1, part * 8 + (1 - odd) * 4 + frame, :] = value[0]
    own = (mine * 8 + line) * 4 + zz
    buf[own] = jnp.where(core == 0, tile32[0], tile32[1]).astype(BF16)

    @pl.when(y == 0)
    def _():
        halo[0] = jnp.zeros((16, 128), BF16)

    @pl.when(y == PLANES - 1)
    def _():
        halo[1] = jnp.zeros((16, 128), BF16)

    partner = at(y, z, member(0, 1))
    last, first = (line == 7) & (y < PLANES - 1), y > 0

    @pl.when(mine == 0)
    def _():
        pl.semaphore_wait(barrier, 13 + 7 * (last | ((line == 0) & first)).astype(jnp.int32))

    @pl.when((mine == 1) & (core == 0))
    def _():
        pl.semaphore_wait(barrier, 9)
        pl.semaphore_signal(known.at[0], inc=1, device_id=partner, device_id_type=MESH)

    @pl.when((mine == 1) & (core == 1))
    def _():
        pl.semaphore_wait(known.at[0], 1)

    @pl.when(mine == 1)
    def _():
        for i in range(4):
            send(buf.at[own], buf.at[own], 0, 7 + zz, at(y, i, line))

    @pl.when((mine == 1) & (core == 1))
    def _():
        pl.semaphore_wait(barrier, 18 + 6 * (last | ((line == 1) & first)).astype(jnp.int32))
        pl.semaphore_signal(known.at[1], inc=1, device_id=partner, device_id_type=MESH)

    @pl.when((mine == 1) & (core == 0))
    def _():
        pl.semaphore_wait(known.at[1], 1)

    def along_x(part, send_at, recv_at):
        block = buf.at[pl.ds((part * 8 + line) * 4, 4)]
        for dx, dc in MEMBERS:
            send(block, block, send_at, recv_at, at(y, z, member(dx, dc)))

    def ends(part):
        @pl.when((part == 0) & (line == 0) & (y > 0))
        def _():
            for i in range(8):
                send(buf.at[0], halo.at[1], 3, 5, at(y - 1, z, i))

        @pl.when((part == 1) & (line == 7) & (y < PLANES - 1))
        def _():
            for i in range(8):
                send(buf.at[63], halo.at[0], 3, 4, at(y + 1, z, i))

    for i in range(1, 4):
        send(buf.at[own], buf.at[own], 0, 0, at(y, mine * 4 + lax.rem(zz + i, 4), line))

    for load in loads[1:]:
        load.start()

    loads[1].wait()
    loads[2].wait()
    for a in range(4):
        for h in range(2):
            i = a * 2 + h
            weight = taper[i : i + 1, :] / math.sqrt(CHANNELS)
            cosine = (weight * coef32[:STRIP, i * 128 : (i + 1) * 128]).astype(BF16)
            sine = (weight * coef32[STRIP:, i * 128 : (i + 1) * 128]).astype(BF16)
            coef[a, :STRIP, h * 128 : (h + 1) * 128] = cosine
            coef[a, STRIP:, h * 128 : (h + 1) * 128] = -sine
            coef[a, :STRIP, 256 + h * 128 : 256 + (h + 1) * 128] = sine
            coef[a, STRIP:, 256 + h * 128 : 256 + (h + 1) * 128] = cosine

    arrived(buf.at[pl.ds(0, 3)], recv_sem.at[0])
    along_x(mine, 1, 2)
    ends(mine)
    low_rows = lax.broadcasted_iota(jnp.int32, (4, 8, 128), 1) < 4

    def arrange(part):
        start = pl.multiple_of(8 + part * HALF_ROWS, 8)
        for p in range(2):
            evens, odds = [], []
            for i in range(4):
                first = buf[pl.ds((part * 8 + 2 * i) * 4, 4)].astype(F32)[:, p * 8 : p * 8 + 8]
                second = buf[pl.ds((part * 8 + 2 * i + 1) * 4, 4)].astype(F32)[:, p * 8 : p * 8 + 8]
                evens.append(jnp.where(low_rows, first, second))
                odds.append(pltpu.roll(jnp.where(low_rows, second, first), 4, 1))
            for h, pieces in enumerate((evens, odds)):
                at_lane = p * 256 + h * 128
                rows32[pl.ds(start, HALF_ROWS), at_lane : at_lane + 128] = jnp.stack(pieces, 1).reshape(HALF_ROWS, 128)

    def short_transforms(part):
        start = pl.multiple_of(8 + part * HALF_ROWS, 8)
        parts = []
        for p in range(2):
            value = rows32[pl.ds(start, HALF_ROWS), p * 256 : (p + 1) * 256].reshape(8, PER_SEG, STRIDE)
            parts.append((value * wins[None]).reshape(HALF_ROWS, STRIDE))
        samples = jnp.concatenate(
            [jnp.concatenate(parts, 1), jnp.concatenate([-parts[1], parts[0]], 1)], 0
        )
        high = samples.astype(BF16)
        low = (samples - high.astype(F32)).astype(BF16)
        turned = (
            jnp.dot(high, turn[0], preferred_element_type=F32)
            + jnp.dot(high, turn[1], preferred_element_type=F32)
            + jnp.dot(low, turn[0], preferred_element_type=F32)
        )
        g_re = turned[:HALF_ROWS].reshape(8, PER_SEG, WIDTH)
        g_im = turned[HALF_ROWS:].reshape(8, PER_SEG, WIDTH)
        cos_step, sin_step = step[0][None], step[1][None]
        for i, value in enumerate((g_re * cos_step + g_im * sin_step, g_im * cos_step - g_re * sin_step)):
            top = value.astype(BF16)
            rhs[pl.ds(part * 8, 8), i * 16 : i * 16 + 16, :] = top
            rhs[pl.ds(part * 8, 8), 32 + i * 16 : 48 + i * 16, :] = (value - top.astype(F32)).astype(BF16)

    def frames(runs):
        pieces = []
        for first, count in runs:
            start = pl.multiple_of(first * PER_SEG, 16)
            pieces.append(rows32[pl.ds(start, (count + 1) * PER_SEG), :].astype(BF16))
        rows = jnp.concatenate(pieces, 0)
        total = None
        for a in range(4):
            term = lax.dot_general(rows, coef[a], (((1,), (1,)), ((), ())), preferred_element_type=F32)
            taken, row = [], 6 + a
            for first, count in runs:
                taken.append(term[row : row + count * PER_SEG])
                row += (count + 1) * PER_SEG
            term = jnp.concatenate(taken, 0)
            total = term if total is None else total + term
        rounded = total.astype(BF16).astype(F32)
        swapped = jnp.concatenate([-rounded[:, STRIP:], rounded[:, :STRIP]], 1)
        row = 0
        for first, count in runs:
            for s in range(count):
                pair = jnp.concatenate([rounded[row : row + PER_SEG], swapped[row : row + PER_SEG]], 0)
                lhs[first + s] = jnp.concatenate([pair, pair], 0).T.astype(BF16)
                row += PER_SEG

    def power(segments, first):
        for n in range(2):
            lanes = slice(n * 256, (n + 1) * 256)
            total = None if first else acc[:, lanes]
            for s in segments:
                e = jnp.dot(lhs[s], rhs[s][:, lanes], preferred_element_type=F32)
                term = e[:STRIP] * e[:STRIP] + e[STRIP:] * e[STRIP:]
                total = term if total is None else total + term
            acc[:, lanes] = total

    def late_tile(i):
        arrived(buf.at[0], recv_sem.at[7 + i])

    def early_block(i):
        block = buf.at[pl.ds(line * 4, 4)]
        send(block, block, 5, 1, at(y, 4 + i, line))

    @pl.when(z == 0)
    def _():
        for i in (3, 2):
            late_tile(i)
            early_block(i)
        late_tile(1)
        late_tile(0)

    @pl.when(z == 3)
    def _():
        for i in (0, 1):
            late_tile(i)
            early_block(i)
        late_tile(2)
        late_tile(3)

    @pl.when((z == 1) | (z == 2))
    def _():
        for i in range(4):
            late_tile(i)

    @pl.when(mine == 1)
    def _():
        arrived(buf.at[pl.ds(0, 4)], recv_sem.at[1])

    along_x(other, 2, 3)
    ends(other)

    for load in loads[3:]:
        load.wait()

    wins = jnp.concatenate(
        [window[pl.ds(0, PER_SEG, stride=2), :], window[pl.ds(1, PER_SEG, stride=2), :]], 1
    ) * (1.0 / 512.0)
    arrived(buf.at[pl.ds(0, 28)], recv_sem.at[2])
    arrange(mine)
    frames([(mine * 8 + 1, 6)])
    short_transforms(mine)
    power([mine * 8 + s for s in range(1, 7)], True)

    arrived(buf.at[pl.ds(0, 28)], recv_sem.at[3])

    @pl.when(y > 0)
    def _():
        arrived(halo.at[0], recv_sem.at[4])

    @pl.when(y < PLANES - 1)
    def _():
        arrived(halo.at[1], recv_sem.at[5])

    before, after = halo[0].astype(F32), halo[1].astype(F32)
    for p in range(2):
        lane = p * 256
        rows32[6:8, lane : lane + 128] = before[p * 8 + 6 : p * 8 + 8]
        rows32[6:8, lane + 128 : lane + 256] = before[p * 8 + 2 : p * 8 + 4]
        rows32[8 + ROWS : 9 + ROWS, lane : lane + 128] = after[p * 8 : p * 8 + 1]
        rows32[8 + ROWS : 9 + ROWS, lane + 128 : lane + 256] = after[p * 8 + 4 : p * 8 + 5]
    arrange(other)
    frames([(mine * 8, 1), (mine * 8 + 7, 1), (other * 8, 8)])
    short_transforms(other)
    power([mine * 8, mine * 8 + 7] + [other * 8 + s for s in range(8)], False)

    low_half = lax.broadcasted_iota(jnp.int32, (16, 8, 256), 1) < 4
    left = acc[:, :256].reshape(16, 8, 256)
    right = acc[:, 256:].reshape(16, 8, 256)
    even = jnp.where(low_half, left, pltpu.roll(right, 4, 1))
    odd = jnp.where(low_half, pltpu.roll(left, 4, 1), right)
    for t in range(16):
        blocks[2 * t] = even[t]
        blocks[2 * t + 1] = odd[t]

    def serve(to, sem):
        send(blocks.at[to], landed.at[place], 4, sem, at(to // 8, z, lax.rem(to, 8)))

    @pl.when(place != FIRST)
    def _():
        serve(FIRST, 11 + y)

    for dy, dx, dc in OWNERS:
        to = ys[dy] * 8 + member(dx, dc)

        @pl.when(to != FIRST)
        def _():
            serve(to, 11 + y)

    landed[place] = blocks[place]
    totals = [None] * LINE
    for dy in (0, 1, 3, 2):
        arrived(landed.at[pl.ds(0, 8 if dy else 7)], recv_sem.at[11 + ys[dy]])
        for i in range(LINE):
            block = landed[ys[dy] * 8 + i]
            totals[i] = block if dy == 0 else totals[i] + block
    for i in range(LINE):
        out[:, i * WIDTH : i * WIDTH + 256] = totals[i][0:4]
        out[:, i * WIDTH + 256 : (i + 1) * WIDTH] = totals[i][4:8]

    @pl.when(mine == 0)
    def _():
        arrived(buf.at[pl.ds(0, 3)], send_sem.at[0])

    @pl.when(mine == 1)
    def _():
        arrived(buf.at[pl.ds(0, 7)], send_sem.at[0])

    @pl.when((z == 0) | (z == 3))
    def _():
        arrived(buf.at[pl.ds(0, 8)], send_sem.at[5])

    arrived(buf.at[pl.ds(0, 28)], send_sem.at[1])
    arrived(buf.at[pl.ds(0, 28)], send_sem.at[2])

    @pl.when((line == 0) & (y > 0))
    def _():
        arrived(buf.at[pl.ds(0, 8)], send_sem.at[3])

    @pl.when((line == 7) & (y < PLANES - 1))
    def _():
        arrived(buf.at[pl.ds(0, 8)], send_sem.at[3])

    arrived(blocks.at[pl.ds(0, 31)], send_sem.at[4])


def body(raw, taper, seg_window):
    channel_table, turn_table, step_table = tables()
    operands = (
        raw, taper.reshape(8, 128), seg_window.reshape(32, 128),
        jnp.asarray(step_table), jnp.asarray(channel_table), jnp.asarray(turn_table),
    )
    vmem = pl.BlockSpec(memory_space=pltpu.VMEM)
    hbm = pl.BlockSpec(memory_space=pltpu.HBM)
    return pl.pallas_call(
        kernel,
        out_shape=jax.ShapeDtypeStruct((4, NFFT), F32),
        in_specs=[hbm] * 6,
        out_specs=vmem,
        scratch_shapes=[
            pltpu.VMEM((2, 1024), BF16),
            pltpu.VMEM((8, 128), F32),
            pltpu.VMEM((32, 128), F32),
            pltpu.VMEM((2, 16, 128), F32),
            pltpu.VMEM((64, 16, 128), BF16),
            pltpu.VMEM((2, 16, 128), BF16),
            pltpu.VMEM((ROWS + 16, 512), F32),
            pltpu.VMEM((2 * STRIP, CHANNELS), F32),
            pltpu.VMEM((4, 2 * STRIP, 512), BF16),
            pltpu.VMEM((2, 512, WIDTH), BF16),
            pltpu.VMEM((2, PER_SEG, WIDTH), F32),
            pltpu.VMEM((PLANE_SEG, 2 * STRIP, 64), BF16),
            pltpu.VMEM((PLANE_SEG, 64, WIDTH), BF16),
            pltpu.VMEM((STRIP, WIDTH), F32),
            pltpu.VMEM((32, 8, 256), F32),
            pltpu.VMEM((32, 8, 256), F32),
            pltpu.SemaphoreType.DMA((6,)),
            pltpu.SemaphoreType.DMA((6,)),
            pltpu.SemaphoreType.DMA((15,)),
            pltpu.SemaphoreType.REGULAR((2,)),
        ],
        compiler_params=pltpu.CompilerParams(
            collective_id=0, has_side_effects=True, vmem_limit_bytes=48 * 1024 * 1024
        ),
    )(*(pltpu.with_memory_space_constraint(x, pltpu.HBM) for x in operands))


def solution(mesh):
    placed = (P(None, ("tm", "grp")), P(), P())
    return jax.shard_map(
        body, mesh=mesh, in_specs=placed, out_specs=P(("tm", "grp"), None), check_vma=False
    )
```

```python
import math

import jax
import jax.numpy as jnp
import numpy as np
from jax import lax
from jax.experimental import pallas as pl
from jax.experimental.pallas import tpu as pltpu
from jax.sharding import PartitionSpec as P

MESH = pl.DeviceIdType.MESH
F32 = jnp.float32
BF16 = jnp.bfloat16

CHANNELS = 1024
NFFT = 4096
STRIDE = 256
PER_SEG = NFFT // STRIDE
SEG = 64
PLANES, DEPTH, LINE = 4, 8, 8
PLANE_SEG = SEG // PLANES
ROWS = PLANE_SEG * PER_SEG
HALF_ROWS = ROWS // 2
STRIP = PLANES * LINE * 4
WIDTH = NFFT // LINE
HOPS = (0, 1, 2, 1)
MEMBERS = sorted(((dx, dc) for dx in range(4) for dc in range(2) if dx or dc), key=lambda m: -HOPS[m[0]])
FIRST = 1


def tables():
    z = np.arange(DEPTH)[:, None, None]
    row = np.arange(STRIP)[None, :, None]
    channel = (row // 32) * 256 + z * 32 + row % 32
    phase = (channel * np.arange(CHANNELS)[None, None, :]) % CHANNELS
    angle = (np.float32(2.0 * math.pi / CHANNELS) * phase.astype(np.float32)).astype(np.float64)
    channel_table = np.concatenate([np.cos(angle), np.sin(angle)], 1).astype(np.float32)
    q = np.arange(LINE)[:, None, None] * WIDTH + np.arange(WIDTH)[None, None, :]
    turn = 2.0 * np.pi / NFFT * ((q * np.arange(STRIDE)[None, :, None]) % NFFT)
    full = np.concatenate([np.cos(turn), -np.sin(turn)], 1)
    high = full.astype(jnp.bfloat16)
    low = (full - high.astype(np.float64)).astype(jnp.bfloat16)
    turn_table = np.stack([high, low], 1)
    j = np.arange(PER_SEG)[:, None]
    step = 2.0 * np.pi / PER_SEG * ((j * np.arange(WIDTH)[None, :]) % PER_SEG)
    step_table = np.stack([np.cos(step), np.sin(step)]).astype(np.float32)
    return channel_table, turn_table, step_table


def kernel(
    raw_hbm, taper_hbm, window_hbm, step_hbm, channel_hbm, turn_hbm, out,
    raw, taper, window, tile32, buf, halo, rows32, coef32, coef, turn, step, lhs, rhs, acc, blocks, landed,
    local_sem, send_sem, recv_sem, known,
):
    tm, grp = lax.axis_index("tm"), lax.axis_index("grp")
    y, z, x_lo = tm // 16, lax.rem(tm // 2, DEPTH), lax.rem(tm, 2)
    x, core = grp // 2 * 2 + x_lo, lax.rem(grp, 2)
    line = x_lo * 4 + grp
    mine, other = z // 4, 1 - z // 4
    zz = lax.rem(z, 4)
    place = y * 8 + line

    xs = [lax.rem(x + d, 4) for d in range(4)]
    ys = [lax.rem(y + d, PLANES) for d in range(PLANES)]
    cores = [core, 1 - core]

    def member(dx, dc):
        return lax.rem(xs[dx], 2) * 4 + xs[dx] // 2 * 2 + cores[dc]

    def at(plane, depth, member):
        return ((plane * DEPTH + depth) * 2 + member // 4, lax.rem(member, 4))

    def send(src, dst, send_at, recv_at, to):
        pltpu.make_async_remote_copy(
            src, dst, send_sem.at[send_at], recv_sem.at[recv_at],
            device_id=to, device_id_type=MESH,
        ).start()

    def arrived(ref, sem):
        pltpu.make_async_copy(ref, ref, sem).wait()

    loads = [
        pltpu.make_async_copy(raw_hbm, raw, local_sem.at[0]),
        pltpu.make_async_copy(taper_hbm, taper, local_sem.at[1]),
        pltpu.make_async_copy(channel_hbm.at[z], coef32, local_sem.at[2]),
        pltpu.make_async_copy(window_hbm, window, local_sem.at[3]),
        pltpu.make_async_copy(step_hbm, step, local_sem.at[4]),
        pltpu.make_async_copy(turn_hbm.at[line], turn, local_sem.at[5]),
    ]
    loads[0].start()

    barrier = pltpu.get_barrier_semaphore()
    even_core, odd_core = line - core, line - core + 1

    def greet(to):
        pl.semaphore_signal(barrier, inc=1, device_id=to, device_id_type=MESH)

    @pl.when(mine == 0)
    def _():
        for i in range(4):
            greet(at(y, 4 + i, even_core))

        @pl.when(z == 0)
        def _():
            for i in range(4):
                greet(at(y, 4 + i, lax.rem(xs[2], 2) * 4 + xs[2] // 2 * 2))

        for i in range(1, 4):
            greet(at(y, lax.rem(zz + i, 4), line))
        for dx, dc in MEMBERS:
            greet(at(y, z, member(dx, dc)))
        for i in range(1, PLANES):
            greet(at(ys[i], z, line))

        @pl.when((y > 0) & (line < 7))
        def _():
            greet(at(y - 1, z, 7))

        @pl.when((y < PLANES - 1) & (line > 0))
        def _():
            greet(at(y + 1, z, 0))

    @pl.when(mine == 1)
    def _():
        @pl.when(core == 1)
        def _():
            greet(at(y, z, even_core))

        for i in range(1, 4):
            greet(at(y, 4 + lax.rem(zz + i, 4), odd_core))
        for dx in (2, 1, 3):
            greet(at(y, z, lax.rem(xs[dx], 2) * 4 + xs[dx] // 2 * 2 + 1))
        for i in range(1, PLANES):
            greet(at(ys[i], z, odd_core))

        @pl.when((y > 0) & (line < 6))
        def _():
            greet(at(y - 1, z, 7))

        @pl.when((y < PLANES - 1) & (line > 1))
        def _():
            greet(at(y + 1, z, 1))

    loads[0].wait()
    pair = raw[...].astype(F32)
    for part in range(2):
        for chunk in range(8):
            odd, frame = chunk % 2, chunk // 2
            value = pair[part : part + 1, chunk * 128 : (chunk + 1) * 128]
            tile32[0, part * 8 + odd * 4 + frame, :] = value[0]
            tile32[1, part * 8 + (1 - odd) * 4 + frame, :] = value[0]
    own = (mine * 8 + line) * 4 + zz
    buf[own] = jnp.where(core == 0, tile32[0], tile32[1]).astype(BF16)

    @pl.when(y == 0)
    def _():
        halo[0] = jnp.zeros((16, 128), BF16)

    @pl.when(y == PLANES - 1)
    def _():
        halo[1] = jnp.zeros((16, 128), BF16)

    partner = at(y, z, member(0, 1))
    last, first = (line == 7) & (y < PLANES - 1), y > 0

    @pl.when(mine == 0)
    def _():
        pl.semaphore_wait(barrier, 13 + 7 * (last | ((line == 0) & first)).astype(jnp.int32))

    @pl.when((mine == 1) & (core == 0))
    def _():
        pl.semaphore_wait(barrier, 11)
        pl.semaphore_signal(known.at[0], inc=1, device_id=partner, device_id_type=MESH)

    @pl.when((mine == 1) & (core == 1))
    def _():
        pl.semaphore_wait(known.at[0], 1)

    @pl.when(mine == 1)
    def _():
        for dc in range(2):
            send(buf.at[own], buf.at[own], 0, 3, at(y, 0, member(2, dc)))
        for i in range(4):
            send(buf.at[own], buf.at[own], 0, 7 + zz, at(y, i, line))

    @pl.when((mine == 1) & (core == 1))
    def _():
        pl.semaphore_wait(barrier, 18 + 6 * (last | ((line == 1) & first)).astype(jnp.int32))
        pl.semaphore_signal(known.at[1], inc=1, device_id=partner, device_id_type=MESH)

    @pl.when((mine == 1) & (core == 0))
    def _():
        pl.semaphore_wait(known.at[1], 1)

    def along_x(part, send_at, recv_at, members):
        block = buf.at[pl.ds((part * 8 + line) * 4, 4)]
        for dx, dc in members:
            send(block, block, send_at, recv_at, at(y, z, member(dx, dc)))

    def ends(part):
        @pl.when((part == 0) & (line == 0) & (y > 0))
        def _():
            for i in range(8):
                send(buf.at[0], halo.at[1], 3, 5, at(y - 1, z, i))

        @pl.when((part == 1) & (line == 7) & (y < PLANES - 1))
        def _():
            for i in range(8):
                send(buf.at[63], halo.at[0], 3, 4, at(y + 1, z, i))

    for i in range(1, 4):
        send(buf.at[own], buf.at[own], 0, 0, at(y, mine * 4 + lax.rem(zz + i, 4), line))

    for load in loads[1:]:
        load.start()

    loads[1].wait()
    loads[2].wait()
    for a in range(4):
        for h in range(2):
            i = a * 2 + h
            weight = taper[i : i + 1, :] / math.sqrt(CHANNELS)
            cosine = (weight * coef32[:STRIP, i * 128 : (i + 1) * 128]).astype(BF16)
            sine = (weight * coef32[STRIP:, i * 128 : (i + 1) * 128]).astype(BF16)
            coef[a, :STRIP, h * 128 : (h + 1) * 128] = cosine
            coef[a, STRIP:, h * 128 : (h + 1) * 128] = -sine
            coef[a, :STRIP, 256 + h * 128 : 256 + (h + 1) * 128] = sine
            coef[a, STRIP:, 256 + h * 128 : 256 + (h + 1) * 128] = cosine

    arrived(buf.at[pl.ds(0, 3)], recv_sem.at[0])
    along_x(mine, 1, 2, MEMBERS)
    ends(mine)
    low_rows = lax.broadcasted_iota(jnp.int32, (4, 8, 128), 1) < 4

    def arrange(part):
        start = pl.multiple_of(8 + part * HALF_ROWS, 8)
        for p in range(2):
            evens, odds = [], []
            for i in range(4):
                first = buf[pl.ds((part * 8 + 2 * i) * 4, 4)].astype(F32)[:, p * 8 : p * 8 + 8]
                second = buf[pl.ds((part * 8 + 2 * i + 1) * 4, 4)].astype(F32)[:, p * 8 : p * 8 + 8]
                evens.append(jnp.where(low_rows, first, second))
                odds.append(pltpu.roll(jnp.where(low_rows, second, first), 4, 1))
            for h, pieces in enumerate((evens, odds)):
                at_lane = p * 256 + h * 128
                rows32[pl.ds(start, HALF_ROWS), at_lane : at_lane + 128] = jnp.stack(pieces, 1).reshape(HALF_ROWS, 128)

    def short_transforms(part):
        start = pl.multiple_of(8 + part * HALF_ROWS, 8)
        parts = []
        for p in range(2):
            value = rows32[pl.ds(start, HALF_ROWS), p * 256 : (p + 1) * 256].reshape(8, PER_SEG, STRIDE)
            parts.append((value * wins[None]).reshape(HALF_ROWS, STRIDE))
        samples = jnp.concatenate(
            [jnp.concatenate(parts, 1), jnp.concatenate([-parts[1], parts[0]], 1)], 0
        )
        high = samples.astype(BF16)
        low = (samples - high.astype(F32)).astype(BF16)
        turned = (
            jnp.dot(high, turn[0], preferred_element_type=F32)
            + jnp.dot(high, turn[1], preferred_element_type=F32)
            + jnp.dot(low, turn[0], preferred_element_type=F32)
        )
        g_re = turned[:HALF_ROWS].reshape(8, PER_SEG, WIDTH)
        g_im = turned[HALF_ROWS:].reshape(8, PER_SEG, WIDTH)
        cos_step, sin_step = step[0][None], step[1][None]
        for i, value in enumerate((g_re * cos_step + g_im * sin_step, g_im * cos_step - g_re * sin_step)):
            top = value.astype(BF16)
            rhs[pl.ds(part * 8, 8), i * 16 : i * 16 + 16, :] = top
            rhs[pl.ds(part * 8, 8), 32 + i * 16 : 48 + i * 16, :] = (value - top.astype(F32)).astype(BF16)

    def frames(runs):
        pieces = []
        for first, count in runs:
            start = pl.multiple_of(first * PER_SEG, 16)
            pieces.append(rows32[pl.ds(start, (count + 1) * PER_SEG), :].astype(BF16))
        rows = jnp.concatenate(pieces, 0)
        total = None
        for a in range(4):
            term = lax.dot_general(rows, coef[a], (((1,), (1,)), ((), ())), preferred_element_type=F32)
            taken, row = [], 6 + a
            for first, count in runs:
                taken.append(term[row : row + count * PER_SEG])
                row += (count + 1) * PER_SEG
            term = jnp.concatenate(taken, 0)
            total = term if total is None else total + term
        rounded = total.astype(BF16).astype(F32)
        swapped = jnp.concatenate([-rounded[:, STRIP:], rounded[:, :STRIP]], 1)
        row = 0
        for first, count in runs:
            for s in range(count):
                pair = jnp.concatenate([rounded[row : row + PER_SEG], swapped[row : row + PER_SEG]], 0)
                lhs[first + s] = jnp.concatenate([pair, pair], 0).T.astype(BF16)
                row += PER_SEG

    def power(segments, first):
        for n in range(2):
            lanes = slice(n * 256, (n + 1) * 256)
            total = None if first else acc[:, lanes]
            for s in segments:
                e = jnp.dot(lhs[s], rhs[s][:, lanes], preferred_element_type=F32)
                term = e[:STRIP] * e[:STRIP] + e[STRIP:] * e[STRIP:]
                total = term if total is None else total + term
            acc[:, lanes] = total

    def late_tile(i):
        arrived(buf.at[0], recv_sem.at[7 + i])

    def early_block(i):
        block = buf.at[pl.ds(line * 4, 4)]
        send(block, block, 5, 1, at(y, 4 + i, line))

    @pl.when(z == 0)
    def _():
        for i in (3, 2):
            late_tile(i)
            early_block(i)
        late_tile(1)
        late_tile(0)

    @pl.when(z == 3)
    def _():
        for i in (0, 1):
            late_tile(i)
            early_block(i)
        late_tile(2)
        late_tile(3)

    @pl.when((z == 1) | (z == 2))
    def _():
        for i in range(4):
            late_tile(i)

    @pl.when(mine == 1)
    def _():
        arrived(buf.at[pl.ds(0, 4)], recv_sem.at[1])

    @pl.when(z > 0)
    def _():
        along_x(other, 2, 3, MEMBERS[:2])

    along_x(other, 2, 3, MEMBERS[2:])
    ends(other)

    for load in loads[3:]:
        load.wait()

    wins = jnp.concatenate(
        [window[pl.ds(0, PER_SEG, stride=2), :], window[pl.ds(1, PER_SEG, stride=2), :]], 1
    ) * (1.0 / 512.0)
    arrived(buf.at[pl.ds(0, 28)], recv_sem.at[2])
    arrange(mine)
    frames([(mine * 8 + 1, 6)])
    short_transforms(mine)
    power([mine * 8 + s for s in range(1, 7)], True)

    arrived(buf.at[pl.ds(0, 28)], recv_sem.at[3])

    @pl.when(y > 0)
    def _():
        arrived(halo.at[0], recv_sem.at[4])

    @pl.when(y < PLANES - 1)
    def _():
        arrived(halo.at[1], recv_sem.at[5])

    before, after = halo[0].astype(F32), halo[1].astype(F32)
    for p in range(2):
        lane = p * 256
        rows32[6:8, lane : lane + 128] = before[p * 8 + 6 : p * 8 + 8]
        rows32[6:8, lane + 128 : lane + 256] = before[p * 8 + 2 : p * 8 + 4]
        rows32[8 + ROWS : 9 + ROWS, lane : lane + 128] = after[p * 8 : p * 8 + 1]
        rows32[8 + ROWS : 9 + ROWS, lane + 128 : lane + 256] = after[p * 8 + 4 : p * 8 + 5]
    arrange(other)
    frames([(mine * 8, 1), (mine * 8 + 7, 1), (other * 8, 8)])
    short_transforms(other)
    rest = [mine * 8, mine * 8 + 7] + [other * 8 + s for s in range(8)]
    low_half = lax.broadcasted_iota(jnp.int32, (4, 8, 256), 1) < 4

    def serve(to):
        send(blocks.at[to], landed.at[place], 4, 11 + y, at(to // 8, z, lax.rem(to, 8)))

    for c in (0, 32, 64, 96):
        lefts = []
        for n in range(2):
            lanes = slice(n * 256, (n + 1) * 256)
            total = acc[c : c + 32, lanes]
            for s in rest:
                pair = jnp.concatenate([lhs[s, c : c + 32], lhs[s, STRIP + c : STRIP + c + 32]], 0)
                e = jnp.dot(pair, rhs[s][:, lanes], preferred_element_type=F32)
                total = total + (e[:32] * e[:32] + e[32:] * e[32:])
            lefts.append(total.reshape(4, 8, 256))
        left, right = lefts
        even = jnp.where(low_half, left, pltpu.roll(right, 4, 1))
        odd = jnp.where(low_half, pltpu.roll(left, 4, 1), right)
        for t in range(4):
            blocks[c // 4 + 2 * t] = even[t]
            blocks[c // 4 + 2 * t + 1] = odd[t]

        if c == 0:

            @pl.when(place != FIRST)
            def _():
                serve(FIRST)

        for dx, dc in MEMBERS + [(0, 0)]:
            to = c // 4 + member(dx, dc)

            @pl.when((to != FIRST) & (to != place))
            def _(to=to):
                serve(to)

    landed[place] = blocks[place]
    totals = [None] * LINE
    for dy in (0, 1, 3, 2):
        arrived(landed.at[pl.ds(0, 8 if dy else 7)], recv_sem.at[11 + ys[dy]])
        for i in range(LINE):
            block = landed[ys[dy] * 8 + i]
            totals[i] = block if dy == 0 else totals[i] + block
    for i in range(LINE):
        out[:, i * WIDTH : i * WIDTH + 256] = totals[i][0:4]
        out[:, i * WIDTH + 256 : (i + 1) * WIDTH] = totals[i][4:8]

    @pl.when(mine == 0)
    def _():
        arrived(buf.at[pl.ds(0, 3)], send_sem.at[0])

    @pl.when(mine == 1)
    def _():
        arrived(buf.at[pl.ds(0, 9)], send_sem.at[0])

    @pl.when((z == 0) | (z == 3))
    def _():
        arrived(buf.at[pl.ds(0, 8)], send_sem.at[5])

    arrived(buf.at[pl.ds(0, 28)], send_sem.at[1])

    @pl.when(z == 0)
    def _():
        arrived(buf.at[pl.ds(0, 20)], send_sem.at[2])

    @pl.when(z > 0)
    def _():
        arrived(buf.at[pl.ds(0, 28)], send_sem.at[2])


    @pl.when((line == 0) & (y > 0))
    def _():
        arrived(buf.at[pl.ds(0, 8)], send_sem.at[3])

    @pl.when((line == 7) & (y < PLANES - 1))
    def _():
        arrived(buf.at[pl.ds(0, 8)], send_sem.at[3])

    arrived(blocks.at[pl.ds(0, 31)], send_sem.at[4])


def body(raw, taper, seg_window):
    channel_table, turn_table, step_table = tables()
    operands = (
        raw, taper.reshape(8, 128), seg_window.reshape(32, 128),
        jnp.asarray(step_table), jnp.asarray(channel_table), jnp.asarray(turn_table),
    )
    vmem = pl.BlockSpec(memory_space=pltpu.VMEM)
    hbm = pl.BlockSpec(memory_space=pltpu.HBM)
    return pl.pallas_call(
        kernel,
        out_shape=jax.ShapeDtypeStruct((4, NFFT), F32),
        in_specs=[hbm] * 6,
        out_specs=vmem,
        scratch_shapes=[
            pltpu.VMEM((2, 1024), BF16),
            pltpu.VMEM((8, 128), F32),
            pltpu.VMEM((32, 128), F32),
            pltpu.VMEM((2, 16, 128), F32),
            pltpu.VMEM((64, 16, 128), BF16),
            pltpu.VMEM((2, 16, 128), BF16),
            pltpu.VMEM((ROWS + 16, 512), F32),
            pltpu.VMEM((2 * STRIP, CHANNELS), F32),
            pltpu.VMEM((4, 2 * STRIP, 512), BF16),
            pltpu.VMEM((2, 512, WIDTH), BF16),
            pltpu.VMEM((2, PER_SEG, WIDTH), F32),
            pltpu.VMEM((PLANE_SEG, 2 * STRIP, 64), BF16),
            pltpu.VMEM((PLANE_SEG, 64, WIDTH), BF16),
            pltpu.VMEM((STRIP, WIDTH), F32),
            pltpu.VMEM((32, 8, 256), F32),
            pltpu.VMEM((32, 8, 256), F32),
            pltpu.SemaphoreType.DMA((6,)),
            pltpu.SemaphoreType.DMA((6,)),
            pltpu.SemaphoreType.DMA((15,)),
            pltpu.SemaphoreType.REGULAR((2,)),
        ],
        compiler_params=pltpu.CompilerParams(
            collective_id=0, has_side_effects=True, vmem_limit_bytes=48 * 1024 * 1024
        ),
    )(*(pltpu.with_memory_space_constraint(x, pltpu.HBM) for x in operands))


def solution(mesh):
    placed = (P(None, ("tm", "grp")), P(), P())
    return jax.shard_map(
        body, mesh=mesh, in_specs=placed, out_specs=P(("tm", "grp"), None), check_vma=False
    )
```

```python
import math

import jax
import jax.numpy as jnp
import numpy as np
from jax import lax
from jax.experimental import pallas as pl
from jax.experimental.pallas import tpu as pltpu
from jax.sharding import PartitionSpec as P

MESH = pl.DeviceIdType.MESH
F32 = jnp.float32
BF16 = jnp.bfloat16

CHANNELS = 1024
NFFT = 4096
STRIDE = 256
PER_SEG = NFFT // STRIDE
SEG = 64
PLANES, DEPTH, LINE = 4, 8, 8
PLANE_SEG = SEG // PLANES
ROWS = PLANE_SEG * PER_SEG
HALF_ROWS = ROWS // 2
STRIP = PLANES * LINE * 4
WIDTH = NFFT // LINE
HOPS = (0, 1, 2, 1)
MEMBERS = sorted(((dx, dc) for dx in range(4) for dc in range(2) if dx or dc), key=lambda m: -HOPS[m[0]])
FIRST = 1


def tables():
    z = np.arange(DEPTH)[:, None, None]
    row = np.arange(STRIP)[None, :, None]
    channel = (row // 32) * 256 + z * 32 + row % 32
    phase = (channel * np.arange(CHANNELS)[None, None, :]) % CHANNELS
    angle = (np.float32(2.0 * math.pi / CHANNELS) * phase.astype(np.float32)).astype(np.float64)
    channel_table = np.concatenate([np.cos(angle), np.sin(angle)], 1).astype(np.float32)
    q = np.arange(LINE)[:, None, None] * WIDTH + np.arange(WIDTH)[None, None, :]
    turn = 2.0 * np.pi / NFFT * ((q * np.arange(STRIDE)[None, :, None]) % NFFT)
    full = np.concatenate([np.cos(turn), -np.sin(turn)], 1)
    high = full.astype(jnp.bfloat16)
    low = (full - high.astype(np.float64)).astype(jnp.bfloat16)
    turn_table = np.stack([high, low], 1)
    j = np.arange(PER_SEG)[:, None]
    step = 2.0 * np.pi / PER_SEG * ((j * np.arange(WIDTH)[None, :]) % PER_SEG)
    step_table = np.stack([np.cos(step), np.sin(step)]).astype(np.float32)
    return channel_table, turn_table, step_table


def kernel(
    raw_hbm, taper_hbm, window_hbm, step_hbm, channel_hbm, turn_hbm, out,
    raw, taper, window, tile32, buf, halo, rows32, coef32, coef, turn, step, lhs, rhs, acc, blocks, landed,
    local_sem, send_sem, recv_sem, known,
):
    tm, grp = lax.axis_index("tm"), lax.axis_index("grp")
    y, z, x_lo = tm // 16, lax.rem(tm // 2, DEPTH), lax.rem(tm, 2)
    x, core = grp // 2 * 2 + x_lo, lax.rem(grp, 2)
    line = x_lo * 4 + grp
    mine, other = z // 4, 1 - z // 4
    zz = lax.rem(z, 4)
    place = y * 8 + line

    xs = [lax.rem(x + d, 4) for d in range(4)]
    ys = [lax.rem(y + d, PLANES) for d in range(PLANES)]
    cores = [core, 1 - core]

    def member(dx, dc):
        return lax.rem(xs[dx], 2) * 4 + xs[dx] // 2 * 2 + cores[dc]

    def at(plane, depth, member):
        return ((plane * DEPTH + depth) * 2 + member // 4, lax.rem(member, 4))

    def send(src, dst, send_at, recv_at, to):
        pltpu.make_async_remote_copy(
            src, dst, send_sem.at[send_at], recv_sem.at[recv_at],
            device_id=to, device_id_type=MESH,
        ).start()

    def arrived(ref, sem):
        pltpu.make_async_copy(ref, ref, sem).wait()

    loads = [
        pltpu.make_async_copy(raw_hbm, raw, local_sem.at[0]),
        pltpu.make_async_copy(taper_hbm, taper, local_sem.at[1]),
        pltpu.make_async_copy(channel_hbm.at[z], coef32, local_sem.at[2]),
        pltpu.make_async_copy(window_hbm, window, local_sem.at[3]),
        pltpu.make_async_copy(step_hbm, step, local_sem.at[4]),
        pltpu.make_async_copy(turn_hbm.at[line], turn, local_sem.at[5]),
    ]
    loads[0].start()

    barrier = pltpu.get_barrier_semaphore()
    even_core, odd_core = line - core, line - core + 1

    def greet(to):
        pl.semaphore_signal(barrier, inc=1, device_id=to, device_id_type=MESH)

    @pl.when(mine == 0)
    def _():
        for i in range(4):
            greet(at(y, 4 + i, even_core))

        @pl.when(z == 0)
        def _():
            for i in range(4):
                greet(at(y, 4 + i, lax.rem(xs[2], 2) * 4 + xs[2] // 2 * 2))

        for i in range(1, 4):
            greet(at(y, lax.rem(zz + i, 4), line))
        for dx, dc in MEMBERS:
            greet(at(y, z, member(dx, dc)))
        for i in range(1, PLANES):
            greet(at(ys[i], z, line))

        @pl.when((y > 0) & (line < 7))
        def _():
            greet(at(y - 1, z, 7))

        @pl.when((y < PLANES - 1) & (line > 0))
        def _():
            greet(at(y + 1, z, 0))

    @pl.when(mine == 1)
    def _():
        @pl.when(core == 1)
        def _():
            greet(at(y, z, even_core))

        for i in range(1, 4):
            greet(at(y, 4 + lax.rem(zz + i, 4), odd_core))
        for dx in (2, 1, 3):
            greet(at(y, z, lax.rem(xs[dx], 2) * 4 + xs[dx] // 2 * 2 + 1))
        for i in range(1, PLANES):
            greet(at(ys[i], z, odd_core))

        @pl.when((y > 0) & (line < 6))
        def _():
            greet(at(y - 1, z, 7))

        @pl.when((y < PLANES - 1) & (line > 1))
        def _():
            greet(at(y + 1, z, 1))

    partner = at(y, z, member(0, 1))

    @pl.when((mine == 1) & (core == 0))
    def _():
        pl.semaphore_wait(barrier, 11)
        pl.semaphore_signal(known.at[0], inc=1, device_id=partner, device_id_type=MESH)

    loads[0].wait()
    pair = raw[...].astype(F32)
    for part in range(2):
        for chunk in range(8):
            odd, frame = chunk % 2, chunk // 2
            value = pair[part : part + 1, chunk * 128 : (chunk + 1) * 128]
            tile32[0, part * 8 + odd * 4 + frame, :] = value[0]
            tile32[1, part * 8 + (1 - odd) * 4 + frame, :] = value[0]
    own = (mine * 8 + line) * 4 + zz
    buf[own] = jnp.where(core == 0, tile32[0], tile32[1]).astype(BF16)

    @pl.when(y == 0)
    def _():
        halo[0] = jnp.zeros((16, 128), BF16)

    @pl.when(y == PLANES - 1)
    def _():
        halo[1] = jnp.zeros((16, 128), BF16)

    last, first = (line == 7) & (y < PLANES - 1), y > 0

    @pl.when(mine == 0)
    def _():
        pl.semaphore_wait(barrier, 13 + 7 * (last | ((line == 0) & first)).astype(jnp.int32))

    @pl.when((mine == 1) & (core == 1))
    def _():
        pl.semaphore_wait(known.at[0], 1)

    @pl.when(mine == 1)
    def _():
        for dc in range(2):
            send(buf.at[own], buf.at[own], 0, 3, at(y, 0, member(2, dc)))
        for i in range(4):
            send(buf.at[own], buf.at[own], 0, 7 + zz, at(y, i, line))

    @pl.when((mine == 1) & (core == 1))
    def _():
        pl.semaphore_wait(barrier, 18 + 6 * (last | ((line == 1) & first)).astype(jnp.int32))
        pl.semaphore_signal(known.at[1], inc=1, device_id=partner, device_id_type=MESH)

    @pl.when((mine == 1) & (core == 0))
    def _():
        pl.semaphore_wait(known.at[1], 1)

    def along_x(part, send_at, recv_at, members):
        block = buf.at[pl.ds((part * 8 + line) * 4, 4)]
        for dx, dc in members:
            send(block, block, send_at, recv_at, at(y, z, member(dx, dc)))

    def ends(part):
        @pl.when((part == 0) & (line == 0) & (y > 0))
        def _():
            for i in range(8):
                send(buf.at[0], halo.at[1], 3, 5, at(y - 1, z, i))

        @pl.when((part == 1) & (line == 7) & (y < PLANES - 1))
        def _():
            for i in range(8):
                send(buf.at[63], halo.at[0], 3, 4, at(y + 1, z, i))

    for i in range(1, 4):
        send(buf.at[own], buf.at[own], 0, 0, at(y, mine * 4 + lax.rem(zz + i, 4), line))

    for load in loads[1:]:
        load.start()

    loads[1].wait()
    loads[2].wait()
    for a in range(4):
        for h in range(2):
            i = a * 2 + h
            weight = taper[i : i + 1, :] / math.sqrt(CHANNELS)
            cosine = (weight * coef32[:STRIP, i * 128 : (i + 1) * 128]).astype(BF16)
            sine = (weight * coef32[STRIP:, i * 128 : (i + 1) * 128]).astype(BF16)
            coef[a, :STRIP, h * 128 : (h + 1) * 128] = cosine
            coef[a, STRIP:, h * 128 : (h + 1) * 128] = -sine
            coef[a, :STRIP, 256 + h * 128 : 256 + (h + 1) * 128] = sine
            coef[a, STRIP:, 256 + h * 128 : 256 + (h + 1) * 128] = cosine

    arrived(buf.at[pl.ds(0, 3)], recv_sem.at[0])
    along_x(mine, 1, 2, MEMBERS)
    ends(mine)
    low_rows = lax.broadcasted_iota(jnp.int32, (4, 8, 128), 1) < 4

    def arrange(part):
        start = pl.multiple_of(8 + part * HALF_ROWS, 8)
        for p in range(2):
            evens, odds = [], []
            for i in range(4):
                first = buf[pl.ds((part * 8 + 2 * i) * 4, 4)].astype(F32)[:, p * 8 : p * 8 + 8]
                second = buf[pl.ds((part * 8 + 2 * i + 1) * 4, 4)].astype(F32)[:, p * 8 : p * 8 + 8]
                evens.append(jnp.where(low_rows, first, second))
                odds.append(pltpu.roll(jnp.where(low_rows, second, first), 4, 1))
            for h, pieces in enumerate((evens, odds)):
                at_lane = p * 256 + h * 128
                rows32[pl.ds(start, HALF_ROWS), at_lane : at_lane + 128] = jnp.stack(pieces, 1).reshape(HALF_ROWS, 128)

    def short_transforms(part):
        start = pl.multiple_of(8 + part * HALF_ROWS, 8)
        parts = []
        for p in range(2):
            value = rows32[pl.ds(start, HALF_ROWS), p * 256 : (p + 1) * 256].reshape(8, PER_SEG, STRIDE)
            parts.append((value * wins[None]).reshape(HALF_ROWS, STRIDE))
        samples = jnp.concatenate(
            [jnp.concatenate(parts, 1), jnp.concatenate([-parts[1], parts[0]], 1)], 0
        )
        high = samples.astype(BF16)
        low = (samples - high.astype(F32)).astype(BF16)
        turned = (
            jnp.dot(high, turn[0], preferred_element_type=F32)
            + jnp.dot(high, turn[1], preferred_element_type=F32)
            + jnp.dot(low, turn[0], preferred_element_type=F32)
        )
        g_re = turned[:HALF_ROWS].reshape(8, PER_SEG, WIDTH)
        g_im = turned[HALF_ROWS:].reshape(8, PER_SEG, WIDTH)
        cos_step, sin_step = step[0][None], step[1][None]
        for i, value in enumerate((g_re * cos_step + g_im * sin_step, g_im * cos_step - g_re * sin_step)):
            top = value.astype(BF16)
            rhs[pl.ds(part * 8, 8), i * 16 : i * 16 + 16, :] = top
            rhs[pl.ds(part * 8, 8), 32 + i * 16 : 48 + i * 16, :] = (value - top.astype(F32)).astype(BF16)

    def frames(runs):
        pieces = []
        for first, count in runs:
            start = pl.multiple_of(first * PER_SEG, 16)
            pieces.append(rows32[pl.ds(start, (count + 1) * PER_SEG), :].astype(BF16))
        rows = jnp.concatenate(pieces, 0)
        total = None
        for a in range(4):
            term = lax.dot_general(rows, coef[a], (((1,), (1,)), ((), ())), preferred_element_type=F32)
            taken, row = [], 6 + a
            for first, count in runs:
                taken.append(term[row : row + count * PER_SEG])
                row += (count + 1) * PER_SEG
            term = jnp.concatenate(taken, 0)
            total = term if total is None else total + term
        rounded = total.astype(BF16).astype(F32)
        swapped = jnp.concatenate([-rounded[:, STRIP:], rounded[:, :STRIP]], 1)
        row = 0
        for first, count in runs:
            for s in range(count):
                pair = jnp.concatenate([rounded[row : row + PER_SEG], swapped[row : row + PER_SEG]], 0)
                lhs[first + s] = jnp.concatenate([pair, pair], 0).T.astype(BF16)
                row += PER_SEG

    def power(segments, first):
        for n in range(2):
            lanes = slice(n * 256, (n + 1) * 256)
            total = None if first else acc[:, lanes]
            for s in segments:
                e = jnp.dot(lhs[s], rhs[s][:, lanes], preferred_element_type=F32)
                term = e[:STRIP] * e[:STRIP] + e[STRIP:] * e[STRIP:]
                total = term if total is None else total + term
            acc[:, lanes] = total

    def late_tile(i):
        arrived(buf.at[0], recv_sem.at[7 + i])

    def early_block(i):
        block = buf.at[pl.ds(line * 4, 4)]
        send(block, block, 5, 1, at(y, 4 + i, line))

    @pl.when(z == 0)
    def _():
        for i in (3, 2):
            late_tile(i)
            early_block(i)
        late_tile(1)
        late_tile(0)

    @pl.when(z == 3)
    def _():
        for i in (0, 1):
            late_tile(i)
            early_block(i)
        late_tile(2)
        late_tile(3)

    @pl.when((z == 1) | (z == 2))
    def _():
        for i in range(4):
            late_tile(i)

    @pl.when(mine == 1)
    def _():
        arrived(buf.at[pl.ds(0, 4)], recv_sem.at[1])

    @pl.when(z > 0)
    def _():
        along_x(other, 2, 3, MEMBERS[:2])

    @pl.when(core == 0)
    def _():
        along_x(other, 2, 3, sorted(MEMBERS[2:], key=lambda m: (m[0] == 0, -m[1], -m[0])))

    @pl.when(core == 1)
    def _():
        along_x(other, 2, 3, sorted(MEMBERS[2:], key=lambda m: (m[0] == 0, m[1], -m[0])))

    ends(other)

    for load in loads[3:]:
        load.wait()

    wins = jnp.concatenate(
        [window[pl.ds(0, PER_SEG, stride=2), :], window[pl.ds(1, PER_SEG, stride=2), :]], 1
    ) * (1.0 / 512.0)
    arrived(buf.at[pl.ds(0, 28)], recv_sem.at[2])
    arrange(mine)
    frames([(mine * 8 + 1, 6)])
    short_transforms(mine)
    power([mine * 8 + s for s in range(1, 7)], True)

    arrived(buf.at[pl.ds(0, 28)], recv_sem.at[3])

    @pl.when(y > 0)
    def _():
        arrived(halo.at[0], recv_sem.at[4])

    @pl.when(y < PLANES - 1)
    def _():
        arrived(halo.at[1], recv_sem.at[5])

    before, after = halo[0].astype(F32), halo[1].astype(F32)
    for p in range(2):
        lane = p * 256
        rows32[6:8, lane : lane + 128] = before[p * 8 + 6 : p * 8 + 8]
        rows32[6:8, lane + 128 : lane + 256] = before[p * 8 + 2 : p * 8 + 4]
        rows32[8 + ROWS : 9 + ROWS, lane : lane + 128] = after[p * 8 : p * 8 + 1]
        rows32[8 + ROWS : 9 + ROWS, lane + 128 : lane + 256] = after[p * 8 + 4 : p * 8 + 5]
    arrange(other)
    frames([(mine * 8, 1), (mine * 8 + 7, 1), (other * 8, 8)])
    short_transforms(other)
    rest = [mine * 8, mine * 8 + 7] + [other * 8 + s for s in range(8)]
    low_half = lax.broadcasted_iota(jnp.int32, (4, 8, 256), 1) < 4

    def serve(to):
        send(blocks.at[to], landed.at[place], 4, 11 + y, at(to // 8, z, lax.rem(to, 8)))

    for c in (0, 32, 64, 96):
        lefts = []
        for n in range(2):
            lanes = slice(n * 256, (n + 1) * 256)
            total = acc[c : c + 32, lanes]
            for s in rest:
                pair = jnp.concatenate([lhs[s, c : c + 32], lhs[s, STRIP + c : STRIP + c + 32]], 0)
                e = jnp.dot(pair, rhs[s][:, lanes], preferred_element_type=F32)
                total = total + (e[:32] * e[:32] + e[32:] * e[32:])
            lefts.append(total.reshape(4, 8, 256))
        left, right = lefts
        even = jnp.where(low_half, left, pltpu.roll(right, 4, 1))
        odd = jnp.where(low_half, pltpu.roll(left, 4, 1), right)
        for t in range(4):
            blocks[c // 4 + 2 * t] = even[t]
            blocks[c // 4 + 2 * t + 1] = odd[t]

        if c == 0:

            @pl.when(place != FIRST)
            def _():
                serve(FIRST)

        for dx, dc in MEMBERS + [(0, 0)]:
            to = c // 4 + member(dx, dc)

            @pl.when((to != FIRST) & (to != place))
            def _(to=to):
                serve(to)

    landed[place] = blocks[place]
    totals = [None] * LINE
    for dy in (0, 1, 3, 2):
        arrived(landed.at[pl.ds(0, 8 if dy else 7)], recv_sem.at[11 + ys[dy]])
        for i in range(LINE):
            block = landed[ys[dy] * 8 + i]
            totals[i] = block if dy == 0 else totals[i] + block
    for i in range(LINE):
        out[:, i * WIDTH : i * WIDTH + 256] = totals[i][0:4]
        out[:, i * WIDTH + 256 : (i + 1) * WIDTH] = totals[i][4:8]

    @pl.when(mine == 0)
    def _():
        arrived(buf.at[pl.ds(0, 3)], send_sem.at[0])

    @pl.when(mine == 1)
    def _():
        arrived(buf.at[pl.ds(0, 9)], send_sem.at[0])

    @pl.when((z == 0) | (z == 3))
    def _():
        arrived(buf.at[pl.ds(0, 8)], send_sem.at[5])

    arrived(buf.at[pl.ds(0, 28)], send_sem.at[1])

    @pl.when(z == 0)
    def _():
        arrived(buf.at[pl.ds(0, 20)], send_sem.at[2])

    @pl.when(z > 0)
    def _():
        arrived(buf.at[pl.ds(0, 28)], send_sem.at[2])


    @pl.when((line == 0) & (y > 0))
    def _():
        arrived(buf.at[pl.ds(0, 8)], send_sem.at[3])

    @pl.when((line == 7) & (y < PLANES - 1))
    def _():
        arrived(buf.at[pl.ds(0, 8)], send_sem.at[3])

    arrived(blocks.at[pl.ds(0, 31)], send_sem.at[4])


def body(raw, taper, seg_window):
    channel_table, turn_table, step_table = tables()
    operands = (
        raw, taper.reshape(8, 128), seg_window.reshape(32, 128),
        jnp.asarray(step_table), jnp.asarray(channel_table), jnp.asarray(turn_table),
    )
    vmem = pl.BlockSpec(memory_space=pltpu.VMEM)
    hbm = pl.BlockSpec(memory_space=pltpu.HBM)
    return pl.pallas_call(
        kernel,
        out_shape=jax.ShapeDtypeStruct((4, NFFT), F32),
        in_specs=[hbm] * 6,
        out_specs=vmem,
        scratch_shapes=[
            pltpu.VMEM((2, 1024), BF16),
            pltpu.VMEM((8, 128), F32),
            pltpu.VMEM((32, 128), F32),
            pltpu.VMEM((2, 16, 128), F32),
            pltpu.VMEM((64, 16, 128), BF16),
            pltpu.VMEM((2, 16, 128), BF16),
            pltpu.VMEM((ROWS + 16, 512), F32),
            pltpu.VMEM((2 * STRIP, CHANNELS), F32),
            pltpu.VMEM((4, 2 * STRIP, 512), BF16),
            pltpu.VMEM((2, 512, WIDTH), BF16),
            pltpu.VMEM((2, PER_SEG, WIDTH), F32),
            pltpu.VMEM((PLANE_SEG, 2 * STRIP, 64), BF16),
            pltpu.VMEM((PLANE_SEG, 64, WIDTH), BF16),
            pltpu.VMEM((STRIP, WIDTH), F32),
            pltpu.VMEM((32, 8, 256), F32),
            pltpu.VMEM((32, 8, 256), F32),
            pltpu.SemaphoreType.DMA((6,)),
            pltpu.SemaphoreType.DMA((6,)),
            pltpu.SemaphoreType.DMA((15,)),
            pltpu.SemaphoreType.REGULAR((2,)),
        ],
        compiler_params=pltpu.CompilerParams(
            collective_id=0, has_side_effects=True, vmem_limit_bytes=48 * 1024 * 1024
        ),
    )(*(pltpu.with_memory_space_constraint(x, pltpu.HBM) for x in operands))


def solution(mesh):
    placed = (P(None, ("tm", "grp")), P(), P())
    return jax.shard_map(
        body, mesh=mesh, in_specs=placed, out_specs=P(("tm", "grp"), None), check_vma=False
    )
```
